32 devices in a mesh: mode: 16 (over z, y, x), col: 2 (over core).
Axes of the slice: x: 2, y: 2, z: 4, core: 2. Of those that a mesh axis runs over, the one named last changes fastest.
Arguments:
- tensor: float32 [512, 4, 4096], P('mode', 'col'), may hold values from -12 to 12, as said below
- initial: float32 [512, 128], replicated, may hold values from -6 to 6
Outputs:
- core_tensor: float32 [128, 4, 4096], P(None, 'col', 'mode')
- basis: float32 [512, 128], replicated
- triangle: float32 [512, 512], replicated
The draws below stay inside these ranges and needn't reach their ends.
Inputs may be any that keep to these rules, and one draw needn't show every extreme that they name: `tensor`: a float field of order one.
All inputs are finite; a program needn't handle non-finite values.
Results may differ from the reference program's by a relative error of at most 0.0003.
Values sent between devices are 32-bit elements; how exact they have to be, the bound alone decides.
No kernel may reach another device: no remote copies, remote signals or barrier semaphores. Data moves between devices by JAX's collectives and lax.ppermute only.
A program may use at most 128 MiB of HBM per device.

```python
import math
import jax
import jax.numpy as jnp
from jax import lax

R = 512
KEEP = 128
ITERS = 3
S_DEV = 2
W_DEV = 256
S = 4
W = 4096


def draw_tensor(key, part):
    keys = jax.random.split(jax.random.fold_in(key, 17), 5)
    noise = jnp.clip(jax.random.normal(keys[0], (R, S, W), jnp.float32), -5.0, 5.0)
    row_scale = jnp.exp(jax.random.uniform(keys[1], (R,), jnp.float32, math.log(0.33), 0.0))
    block_amp = jnp.exp(jax.random.uniform(keys[2], (S // S_DEV, W // W_DEV), jnp.float32, math.log(0.1), 0.0))
    block_corr = jax.random.uniform(keys[3], (S // S_DEV, W // W_DEV), jnp.float32, 0.1, 0.45)
    amp_full = jnp.repeat(jnp.repeat(block_amp, S_DEV, 0), W_DEV, 1)
    corr_full = jnp.repeat(jnp.repeat(block_corr, S_DEV, 0), W_DEV, 1)
    rough = jax.random.uniform(keys[4], (S, W), jnp.float32, 0.5, 1.5)
    shifted = jnp.concatenate([jnp.zeros((1, S, W), jnp.float32), noise[:-1]], 0)
    mixed = noise + corr_full[None] * shifted
    return row_scale[:, None, None] * (amp_full * rough)[None] * mixed


def gaussian(rng, extent, spread, most, kind=jnp.bfloat16):
    return jnp.clip(spread * jax.random.normal(rng, extent, jnp.float32), -most, most).astype(kind)


def setup_inputs(seed: int = 0) -> dict:
    key_list = jax.random.split(jax.random.key(seed), 3)
    tensor = draw_tensor(jax.random.fold_in(key_list[2], 71), 0)
    initial = gaussian(key_list[1], (R, KEEP), 1.0, 6.0, jnp.float32)
    return dict(tensor=tensor, initial=initial)


precise = lax.Precision.HIGHEST

def reference(tensor, initial):
    column_count = S * W
    unfold = tensor.reshape(R, column_count)
    gram = jnp.dot(unfold.astype(jnp.float32), unfold.T.astype(jnp.float32), precision=precise, preferred_element_type=jnp.float32) / column_count
    triangle = jnp.linalg.cholesky(gram).T
    current = initial
    for sweep in range(ITERS):
        product = jnp.dot(gram.astype(jnp.float32), current.astype(jnp.float32), precision=precise, preferred_element_type=jnp.float32)
        inner = jnp.dot(product.T.astype(jnp.float32), product.astype(jnp.float32), precision=precise, preferred_element_type=jnp.float32)
        lower_factor = jnp.linalg.cholesky(inner)
        current = lax.linalg.triangular_solve(lower_factor, product, left_side=False, lower=True, transpose_a=True)
    core_flat = jnp.dot(current.T.astype(jnp.float32), unfold.astype(jnp.float32), precision=precise, preferred_element_type=jnp.float32)
    return (core_flat.reshape(KEEP, S, W), current, triangle)
```

```python
import jax
import jax.numpy as jnp
from jax import lax
from jax.sharding import PartitionSpec as P

ITERS = 3
TILE = 128

precise = lax.Precision.HIGHEST


def matmul(left, right):
    return jnp.dot(left, right, precision=precise, preferred_element_type=jnp.float32)


def exchanged(value, axis, distance):
    pairs = [(source, source ^ distance) for source in range(lax.axis_size(axis))]
    return lax.ppermute(value, axis, pairs)


def scattered_sum(value, axis, group):
    place = lax.axis_index(axis) % group
    rows = value.shape[0] // group
    total = lax.dynamic_slice_in_dim(value, place * rows, rows)
    parts = [
        exchanged(lax.dynamic_slice_in_dim(value, (place ^ distance) * rows, rows), axis, distance)
        for distance in range(1, group)
    ]
    for part in parts:
        total = total + part
    return total


def gathered(value, axis, group):
    place = lax.axis_index(axis) % group
    rows = value.shape[0]
    whole = jnp.zeros((group * rows,) + value.shape[1:], value.dtype)
    whole = lax.dynamic_update_slice_in_dim(whole, value, place * rows, 0)
    for distance in range(1, group):
        part = exchanged(value, axis, distance)
        whole = lax.dynamic_update_slice_in_dim(whole, part, (place ^ distance) * rows, 0)
    return whole


def summed(value):
    mode_size, col_size = lax.axis_size("mode"), lax.axis_size("col")
    col_group = min(2, col_size)
    mode_group = min(4, mode_size)
    value = scattered_sum(value, "col", col_group)
    value = scattered_sum(value, "mode", mode_group)
    distance = mode_group
    while distance < mode_size:
        value = value + exchanged(value, "mode", distance)
        distance *= 2
    distance = col_group
    while distance < col_size:
        value = value + exchanged(value, "col", distance)
        distance *= 2
    value = gathered(value, "mode", mode_group)
    return gathered(value, "col", col_group)


def local(tensor, initial):
    mode_size = lax.axis_size("mode")
    row_part, slab_count, width = tensor.shape
    cell_count = width // mode_size
    row_count = row_part * mode_size
    column_total = slab_count * width * lax.axis_size("col")
    blocks = tensor.reshape(row_part, slab_count, mode_size, cell_count).transpose(2, 0, 1, 3)
    blocks = blocks.reshape(mode_size, row_part, slab_count * cell_count)
    regrouped = lax.all_to_all(blocks, "mode", split_axis=0, concat_axis=0, tiled=True)
    unfold = regrouped.reshape(row_count, slab_count * cell_count)
    local_gram = matmul(unfold, unfold.T) / column_total
    tiles = row_count // TILE
    packed = jnp.concatenate(
        [
            local_gram[i * TILE : (i + 1) * TILE, j * TILE : (j + 1) * TILE]
            for i in range(tiles)
            for j in range(i, tiles)
        ]
    )
    packed = summed(packed)
    found = {}
    for i in range(tiles):
        for j in range(i, tiles):
            start = len(found) * TILE
            found[i, j] = packed[start : start + TILE]
    gram_sum = jnp.concatenate(
        [
            jnp.concatenate([found[i, j] if i <= j else found[j, i].T for j in range(tiles)], 1)
            for i in range(tiles)
        ]
    )
    triangle = jnp.linalg.cholesky(gram_sum).T
    current = initial
    for sweep in range(ITERS):
        product = matmul(gram_sum, current)
        inner = matmul(product.T, product)
        lower_factor = jnp.linalg.cholesky(inner)
        current = lax.linalg.triangular_solve(
            lower_factor, product, left_side=False, lower=True, transpose_a=True
        )
    core_flat = matmul(current.T, unfold)
    core_tensor = core_flat.reshape(current.shape[1], slab_count, cell_count)
    return (core_tensor, current, triangle)


def solution(mesh):
    return jax.shard_map(
        local,
        mesh=mesh,
        in_specs=(P("mode", "col", None), P()),
        out_specs=(P(None, "col", "mode"), P(), P()),
        check_vma=False,
    )
```

```python
import functools

import jax
import jax.numpy as jnp
from jax import lax
from jax.experimental import pallas as pl
from jax.experimental.pallas import tpu as pltpu
from jax.sharding import PartitionSpec as P

ITERS = 3
TILE = 128
SUB = 8
PANEL = 2

precise = lax.Precision.HIGHEST


def matmul(left, right):
    return jnp.dot(left, right, precision=precise, preferred_element_type=jnp.float32)


def matmul_tn(left, right):
    return lax.dot_general(
        left, right, (((0,), (0,)), ((), ())), precision=precise, preferred_element_type=jnp.float32
    )


def matmul_nt(left, right):
    return lax.dot_general(
        left, right, (((1,), (1,)), ((), ())), precision=precise, preferred_element_type=jnp.float32
    )


def exchanged(value, axis, distance):
    pairs = [(source, source ^ distance) for source in range(lax.axis_size(axis))]
    return lax.ppermute(value, axis, pairs)


def scattered_sum(value, axis, group):
    place = lax.axis_index(axis) % group
    rows = value.shape[0] // group
    total = lax.dynamic_slice_in_dim(value, place * rows, rows)
    parts = [
        exchanged(lax.dynamic_slice_in_dim(value, (place ^ distance) * rows, rows), axis, distance)
        for distance in range(1, group)
    ]
    for part in parts:
        total = total + part
    return total


def gathered(value, axis, group):
    place = lax.axis_index(axis) % group
    rows = value.shape[0]
    whole = jnp.zeros((group * rows,) + value.shape[1:], value.dtype)
    whole = lax.dynamic_update_slice_in_dim(whole, value, place * rows, 0)
    for distance in range(1, group):
        part = exchanged(value, axis, distance)
        whole = lax.dynamic_update_slice_in_dim(whole, part, (place ^ distance) * rows, 0)
    return whole


def summed(value):
    mode_size, col_size = lax.axis_size("mode"), lax.axis_size("col")
    col_group = min(2, col_size)
    mode_group = min(4, mode_size)
    value = scattered_sum(value, "col", col_group)
    value = scattered_sum(value, "mode", mode_group)
    distance = mode_group
    while distance < mode_size:
        value = value + exchanged(value, "mode", distance)
        distance *= 2
    distance = col_group
    while distance < col_size:
        value = value + exchanged(value, "col", distance)
        distance *= 2
    value = gathered(value, "mode", mode_group)
    return gathered(value, "col", col_group)


def row_of(tile, index):
    return jnp.broadcast_to(tile[index : index + 1, :], tile.shape)


def lane_of(tile, index):
    return jnp.take_along_axis(tile, jnp.full(tile.shape, index, jnp.int32), axis=1)


def factored(block, with_upper):
    side = block.shape[0]
    count = side // SUB
    width = PANEL * SUB
    row = lax.broadcasted_iota(jnp.int32, (SUB, side), 0)
    lane = lax.broadcasted_iota(jnp.int32, (SUB, side), 1)
    tiles = [block[SUB * t : SUB * t + SUB, :] for t in range(count)]
    scales = [None] * count
    for first in range(0, count, PANEL):
        base = first * SUB
        inside = (lane >= base) & (lane < base + width)
        members = range(PANEL)
        columns = [[lane_of(tiles[first + h], base + j) for h in members] for j in range(width)]
        below = {
            t: [lane_of(tiles[t], base + j) for j in range(width)] for t in range(first + PANEL, count)
        }
        upper = [tiles[first + h] for h in members]
        inverse = [
            jnp.where(inside, jnp.where(lane == row + base + SUB * h, 1.0, 0.0), upper[h]) for h in members
        ]
        kept_upper, kept_inverse, scale = list(upper), list(inverse), [None] * PANEL
        for pivot in range(width):
            own, place = divmod(pivot, SUB)
            reciprocal = pl.reciprocal(row_of(columns[pivot][own], place), approx=True)
            first_row = place == 0
            here = row == place
            scale[own] = reciprocal if first_row else jnp.where(here, reciprocal, scale[own])
            kept_inverse[own] = inverse[own] if first_row else jnp.where(here, inverse[own], kept_inverse[own])
            if with_upper:
                kept_upper[own] = upper[own] if first_row else jnp.where(here, upper[own], kept_upper[own])
            factor = [
                (jnp.where(here, 0.0, columns[pivot][h]) if h == own else columns[pivot][h]) * reciprocal
                for h in members
            ]
            for j in range(pivot + 1, width):
                value = row_of(columns[j][own], place)
                columns[j] = [columns[j][h] - factor[h] * value for h in members]
            value = row_of(inverse[own], place)
            inverse = [inverse[h] - factor[h] * value for h in members]
            if with_upper:
                value = row_of(upper[own], place)
                upper = [upper[h] - factor[h] * value for h in members]
        for h in members:
            on_or_right = inside & (lane >= row + base + SUB * h)
            tiles[first + h] = (
                jnp.where(on_or_right, kept_upper[h], kept_inverse[h]) if with_upper else kept_inverse[h]
            )
            scales[first + h] = scale[h]
        if first + PANEL < count:
            reduced = [inverse[h] * scale[h] for h in members]
            rows = [row_of(reduced[m // SUB], m % SUB) for m in range(width)]
            for t in range(first + PANEL, count):
                even = jnp.where(inside, 0.0, tiles[t])
                odd = None
                for m in range(width):
                    term = below[t][m] * rows[m]
                    if m % 2:
                        odd = term if odd is None else odd + term
                    else:
                        even = even - term
                tiles[t] = even - odd
    uppers, inverses = [], []
    for t in range(count):
        root = lax.rsqrt(scales[t]) * scales[t]
        scaled = tiles[t] * root
        diagonal = row + SUB * t
        uppers.append(jnp.where(lane >= diagonal, scaled, 0.0))
        inverses.append(jnp.where(lane < diagonal, scaled, jnp.where(lane == diagonal, root, 0.0)))
    return (jnp.concatenate(uppers) if with_upper else None), jnp.concatenate(inverses)


def block_places(tiles):
    return {
        pair: place for place, pair in enumerate((i, j) for i in range(tiles) for j in range(i, tiles))
    }


def write_triangle(packed_ref, triangle_ref):
    tiles = triangle_ref.shape[0] // TILE
    places = block_places(tiles)
    blocks = {pair: packed_ref[TILE * at : TILE * at + TILE, :] for pair, at in places.items()}
    for k in range(tiles):
        upper, inverse = factored(blocks[k, k], True)
        for j in range(tiles):
            if j < k:
                part = jnp.zeros((TILE, TILE), jnp.float32)
            elif j == k:
                part = upper
            else:
                part = blocks[k, j] = matmul(inverse, blocks[k, j])
            triangle_ref[TILE * k : TILE * k + TILE, TILE * j : TILE * j + TILE] = part
        for i in range(k + 1, tiles):
            for j in range(i, tiles):
                blocks[i, j] = blocks[i, j] - matmul_tn(blocks[k, i], blocks[k, j])


def write_basis(packed_ref, initial_ref, basis_ref, gram_ref):
    tiles = gram_ref.shape[0] // TILE
    for (i, j), at in block_places(tiles).items():
        block = packed_ref[TILE * at : TILE * at + TILE, :]
        gram_ref[TILE * i : TILE * i + TILE, TILE * j : TILE * j + TILE] = block
        if i != j:
            gram_ref[TILE * j : TILE * j + TILE, TILE * i : TILE * i + TILE] = block.T
    product_t = matmul(initial_ref[...].T, gram_ref[...])
    for sweep in range(ITERS):
        inner = matmul_nt(product_t, product_t)
        if sweep < ITERS - 1:
            following = matmul(product_t, gram_ref[...])
        _, inverse = factored(inner, False)
        if sweep < ITERS - 1:
            product_t = matmul(inverse, following)
    basis_ref[...] = matmul(inverse, product_t).T


def factor_kernel(part_ref, packed_ref, initial_ref, triangle_ref, basis_ref, gram_ref):
    @pl.when(part_ref[0] != 1)
    def _():
        write_triangle(packed_ref, triangle_ref)

    @pl.when(part_ref[0] != 0)
    def _():
        write_basis(packed_ref, initial_ref, basis_ref, gram_ref)


def factors(packed, initial):
    rows, keep = initial.shape
    col_size = lax.axis_size("col")
    shared = col_size % 2 == 0
    part = lax.axis_index("col") % 2 if shared else jnp.int32(2)
    vmem = pl.BlockSpec(memory_space=pltpu.VMEM)
    triangle, basis = pl.pallas_call(
        factor_kernel,
        out_shape=[
            jax.ShapeDtypeStruct((rows, rows), jnp.float32),
            jax.ShapeDtypeStruct((rows, keep), jnp.float32),
        ],
        in_specs=[pl.BlockSpec(memory_space=pltpu.SMEM), vmem, vmem],
        out_specs=[vmem, vmem],
        scratch_shapes=[pltpu.VMEM((rows, rows), jnp.float32)],
        compiler_params=pltpu.CompilerParams(vmem_limit_bytes=32 * 2**20),
    )(jnp.full((1,), part, jnp.int32), packed, initial)
    if not shared:
        return triangle, basis
    got_basis = lax.ppermute(basis, "col", [(d + 1, d) for d in range(0, col_size, 2)])
    got_triangle = lax.ppermute(triangle, "col", [(d, d + 1) for d in range(0, col_size, 2)])
    return jnp.where(part == 0, triangle, got_triangle), jnp.where(part == 0, got_basis, basis)


def local(tensor, initial):
    mode_size = lax.axis_size("mode")
    row_part, slab_count, width = tensor.shape
    cell_count = width // mode_size
    row_count = row_part * mode_size
    column_total = slab_count * width * lax.axis_size("col")
    blocks = tensor.reshape(row_part, slab_count, mode_size, cell_count).transpose(2, 0, 1, 3)
    blocks = blocks.reshape(mode_size, row_part, slab_count * cell_count)
    regrouped = lax.all_to_all(blocks, "mode", split_axis=0, concat_axis=0, tiled=True)
    unfold = regrouped.reshape(row_count, slab_count * cell_count)
    local_gram = matmul(unfold, unfold.T) / column_total
    packed = jnp.concatenate(
        [
            local_gram[i * TILE : (i + 1) * TILE, j * TILE : (j + 1) * TILE]
            for i, j in block_places(row_count // TILE)
        ]
    )
    triangle, current = factors(summed(packed), initial)
    core_flat = matmul(current.T, unfold)
    core_tensor = core_flat.reshape(current.shape[1], slab_count, cell_count)
    return (core_tensor, current, triangle)


def solution(mesh):
    return jax.shard_map(
        local,
        mesh=mesh,
        in_specs=(P("mode", "col", None), P()),
        out_specs=(P(None, "col", "mode"), P(), P()),
        check_vma=False,
    )
```

```python
import functools

import jax
import jax.numpy as jnp
from jax import lax
from jax.experimental import pallas as pl
from jax.experimental.pallas import tpu as pltpu
from jax.sharding import PartitionSpec as P

ITERS = 3
TILE = 128
SUB = 8
PANEL = 2

precise = lax.Precision.HIGHEST


def matmul(left, right):
    return jnp.dot(left, right, precision=precise, preferred_element_type=jnp.float32)


def matmul_tn(left, right):
    return lax.dot_general(
        left, right, (((0,), (0,)), ((), ())), precision=precise, preferred_element_type=jnp.float32
    )


def matmul_nt(left, right):
    return lax.dot_general(
        left, right, (((1,), (1,)), ((), ())), precision=precise, preferred_element_type=jnp.float32
    )


def exchanged(value, axis, distance):
    pairs = [(source, source ^ distance) for source in range(lax.axis_size(axis))]
    return lax.ppermute(value, axis, pairs)


def scattered_sum(value, axis, group):
    place = lax.axis_index(axis) % group
    rows = value.shape[0] // group
    total = lax.dynamic_slice_in_dim(value, place * rows, rows)
    parts = [
        exchanged(lax.dynamic_slice_in_dim(value, (place ^ distance) * rows, rows), axis, distance)
        for distance in range(1, group)
    ]
    for part in parts:
        total = total + part
    return total


def gathered(value, axis, group):
    place = lax.axis_index(axis) % group
    rows = value.shape[0]
    whole = jnp.zeros((group * rows,) + value.shape[1:], value.dtype)
    whole = lax.dynamic_update_slice_in_dim(whole, value, place * rows, 0)
    for distance in range(1, group):
        part = exchanged(value, axis, distance)
        whole = lax.dynamic_update_slice_in_dim(whole, part, (place ^ distance) * rows, 0)
    return whole


def summed(value):
    mode_size, col_size = lax.axis_size("mode"), lax.axis_size("col")
    col_group = min(2, col_size)
    mode_group = min(4, mode_size)
    value = scattered_sum(value, "col", col_group)
    value = scattered_sum(value, "mode", mode_group)
    distance = mode_group
    while distance < mode_size:
        value = value + exchanged(value, "mode", distance)
        distance *= 2
    distance = col_group
    while distance < col_size:
        value = value + exchanged(value, "col", distance)
        distance *= 2
    value = gathered(value, "mode", mode_group)
    return gathered(value, "col", col_group)


def row_of(tile, index):
    return jnp.broadcast_to(tile[index : index + 1, :], tile.shape)


def lane_of(tile, index):
    return jnp.take_along_axis(tile, jnp.full(tile.shape, index, jnp.int32), axis=1)


def factored(block, with_upper):
    side = block.shape[0]
    count = side // SUB
    width = PANEL * SUB
    row = lax.broadcasted_iota(jnp.int32, (SUB, side), 0)
    lane = lax.broadcasted_iota(jnp.int32, (SUB, side), 1)
    tiles = [block[SUB * t : SUB * t + SUB, :] for t in range(count)]
    scales = [None] * count
    members = range(PANEL)
    for first in range(0, count, PANEL):
        base = first * SUB
        inside = (lane >= base) & (lane < base + width)
        columns = [[lane_of(tiles[first + h], base + j) for h in members] for j in range(width)]
        near = range(first + PANEL, min(first + 2 * PANEL, count))
        far = range(first + 2 * PANEL, count)
        below = {t: [lane_of(tiles[t], base + j) for j in range(width)] for t in near}
        panel = [tiles[first + h] for h in members]
        if far:
            sent = jnp.concatenate([jnp.where(lane >= base + width + width, panel[h], 0.0) for h in members])
        kept, scale = list(panel), [None] * PANEL
        for pivot in range(width):
            own, place = divmod(pivot, SUB)
            here = row == place
            cleared = lane == base + pivot
            reciprocal = pl.reciprocal(row_of(columns[pivot][own], place), approx=True)
            scale[own] = jnp.where(here, reciprocal, scale[own]) if place else reciprocal
            kept[own] = jnp.where(here, panel[own], kept[own]) if place else panel[own]
            factor = [
                (jnp.where(here, 0.0, columns[pivot][h]) if h == own else columns[pivot][h]) * reciprocal
                for h in members
            ]
            for j in range(pivot + 1, width):
                value = row_of(columns[j][own], place)
                columns[j] = [columns[j][h] - factor[h] * value for h in members]
            value = jnp.where(cleared, 1.0, row_of(panel[own], place))
            panel = [
                jnp.where(cleared, jnp.where(here, 1.0, 0.0) if h == own else 0.0, panel[h]) - factor[h] * value
                for h in members
            ]
        for h in members:
            tiles[first + h] = kept[h]
            scales[first + h] = scale[h]
        if near:
            reduced = [panel[h] * scale[h] for h in members]
            rows = [row_of(reduced[m // SUB], m % SUB) for m in range(width)]
            for t in near:
                even = jnp.where(inside, 0.0, tiles[t])
                odd = None
                for m in range(width):
                    term = below[t][m] * rows[m]
                    if m % 2:
                        odd = term if odd is None else odd + term
                    else:
                        even = even - term
                tiles[t] = even - odd
            if far:
                update = matmul_tn(sent, jnp.concatenate(reduced))
                for t in far:
                    tiles[t] = jnp.where(inside, 0.0, tiles[t]) - update[SUB * t : SUB * t + SUB]
    uppers, inverses = [], []
    for t in range(count):
        root = lax.rsqrt(scales[t]) * scales[t]
        scaled = tiles[t] * root
        diagonal = row + SUB * t
        uppers.append(jnp.where(lane >= diagonal, scaled, 0.0))
        inverses.append(jnp.where(lane < diagonal, scaled, jnp.where(lane == diagonal, root, 0.0)))
    return (jnp.concatenate(uppers) if with_upper else None), jnp.concatenate(inverses)


def block_places(tiles):
    return {
        pair: place for place, pair in enumerate((i, j) for i in range(tiles) for j in range(i, tiles))
    }


def write_triangle(packed_ref, outbox_ref, tiles):
    places = block_places(tiles)
    blocks = {pair: packed_ref[TILE * at : TILE * at + TILE, :] for pair, at in places.items()}
    for k in range(tiles):
        blocks[k, k], inverse = factored(blocks[k, k], True)
        for j in range(k + 1, tiles):
            blocks[k, j] = matmul(inverse, blocks[k, j])
        for j in range(k, tiles):
            at = places[k, j]
            outbox_ref[TILE * at : TILE * at + TILE, :] = blocks[k, j]
        for i in range(k + 1, tiles):
            for j in range(i, tiles):
                blocks[i, j] = blocks[i, j] - matmul_tn(blocks[k, i], blocks[k, j])


def write_basis(packed_ref, initial_ref, outbox_ref, gram_ref, tiles):
    for (i, j), at in block_places(tiles).items():
        block = packed_ref[TILE * at : TILE * at + TILE, :]
        gram_ref[TILE * i : TILE * i + TILE, TILE * j : TILE * j + TILE] = block
        if i != j:
            gram_ref[TILE * j : TILE * j + TILE, TILE * i : TILE * i + TILE] = block.T
    product_t = matmul(initial_ref[...].T, gram_ref[...])
    for sweep in range(ITERS):
        inner = matmul_nt(product_t, product_t)
        if sweep < ITERS - 1:
            following = matmul(product_t, gram_ref[...])
        _, inverse = factored(inner, False)
        if sweep < ITERS - 1:
            product_t = matmul(inverse, following)
    current_t = matmul(inverse, product_t)
    rows = current_t.shape[1]
    outbox_ref[:rows, :] = current_t.T
    for i in range(tiles):
        outbox_ref[rows + TILE * i : rows + TILE * i + TILE, :] = current_t[:, TILE * i : TILE * i + TILE]


def factor_kernel(tiles, part_ref, packed_ref, initial_ref, outbox_ref, gram_ref):
    @pl.when(part_ref[0] == 0)
    def _():
        write_triangle(packed_ref, outbox_ref, tiles)

    @pl.when(part_ref[0] != 0)
    def _():
        write_basis(packed_ref, initial_ref, outbox_ref, gram_ref, tiles)


def closing_kernel(tiles, part_ref, outbox_ref, inbox_ref, unfold_ref, core_ref, basis_ref, triangle_ref):
    def close(triangle_box, basis_box):
        places = block_places(tiles)
        rows = basis_ref.shape[0]
        current_t = jnp.concatenate(
            [basis_box[rows + TILE * i : rows + TILE * i + TILE, :] for i in range(tiles)], axis=1
        )
        core_ref[...] = matmul(current_t, unfold_ref[...])
        basis_ref[...] = basis_box[:rows, :]
        for i in range(tiles):
            for j in range(tiles):
                at = places.get((i, j))
                triangle_ref[TILE * i : TILE * i + TILE, TILE * j : TILE * j + TILE] = (
                    jnp.zeros((TILE, TILE), jnp.float32)
                    if at is None
                    else triangle_box[TILE * at : TILE * at + TILE, :]
                )

    @pl.when(part_ref[0] == 0)
    def _():
        close(outbox_ref, inbox_ref)

    @pl.when(part_ref[0] != 0)
    def _():
        close(inbox_ref, outbox_ref)


VMEM_LIMIT = 32 * 2**20


def factors(packed, initial, part):
    rows, keep = initial.shape
    tiles = rows // TILE
    vmem = pl.BlockSpec(memory_space=pltpu.VMEM)
    return pl.pallas_call(
        functools.partial(factor_kernel, tiles),
        out_shape=jax.ShapeDtypeStruct((max(packed.shape[0], rows + tiles * keep), TILE), jnp.float32),
        in_specs=[pl.BlockSpec(memory_space=pltpu.SMEM), vmem, vmem],
        out_specs=vmem,
        scratch_shapes=[pltpu.VMEM((rows, rows), jnp.float32)],
        compiler_params=pltpu.CompilerParams(vmem_limit_bytes=VMEM_LIMIT),
    )(part, packed, initial)


def finished(packed, initial, unfold):
    rows, keep = initial.shape
    if lax.axis_size("col") % 2 == 0:
        part = jnp.full((1,), lax.axis_index("col") % 2, jnp.int32)
        outbox = factors(packed, initial, part)
        inbox = exchanged(outbox, "col", 1)
    else:
        part = jnp.zeros((1,), jnp.int32)
        outbox = factors(packed, initial, part)
        inbox = factors(packed, initial, part + 1)
    vmem = pl.BlockSpec(memory_space=pltpu.VMEM)
    return pl.pallas_call(
        functools.partial(closing_kernel, rows // TILE),
        out_shape=[
            jax.ShapeDtypeStruct((keep, unfold.shape[1]), jnp.float32),
            jax.ShapeDtypeStruct((rows, keep), jnp.float32),
            jax.ShapeDtypeStruct((rows, rows), jnp.float32),
        ],
        in_specs=[pl.BlockSpec(memory_space=pltpu.SMEM), vmem, vmem, vmem],
        out_specs=[vmem, vmem, vmem],
        compiler_params=pltpu.CompilerParams(vmem_limit_bytes=VMEM_LIMIT),
    )(part, outbox, inbox, unfold)


def local(tensor, initial):
    mode_size = lax.axis_size("mode")
    row_part, slab_count, width = tensor.shape
    cell_count = width // mode_size
    row_count = row_part * mode_size
    column_total = slab_count * width * lax.axis_size("col")
    blocks = tensor.reshape(row_part, slab_count, mode_size, cell_count).transpose(2, 0, 1, 3)
    blocks = blocks.reshape(mode_size, row_part, slab_count * cell_count)
    regrouped = lax.all_to_all(blocks, "mode", split_axis=0, concat_axis=0, tiled=True)
    unfold = regrouped.reshape(row_count, slab_count * cell_count)
    local_gram = matmul(unfold, unfold.T) / column_total
    packed = jnp.concatenate(
        [
            local_gram[i * TILE : (i + 1) * TILE, j * TILE : (j + 1) * TILE]
            for i, j in block_places(row_count // TILE)
        ]
    )
    core_flat, current, triangle = finished(summed(packed), initial, unfold)
    core_tensor = core_flat.reshape(current.shape[1], slab_count, cell_count)
    return (core_tensor, current, triangle)


def solution(mesh):
    return jax.shard_map(
        local,
        mesh=mesh,
        in_specs=(P("mode", "col", None), P()),
        out_specs=(P(None, "col", "mode"), P(), P()),
        check_vma=False,
    )
```

```python
import functools

import jax
import jax.numpy as jnp
from jax import lax
from jax.experimental import pallas as pl
from jax.experimental.pallas import tpu as pltpu
from jax.sharding import PartitionSpec as P

ITERS = 3
TILE = 128
SUB = 8
PANEL = 2

precise = lax.Precision.HIGHEST


def matmul(left, right):
    return jnp.dot(left, right, precision=precise, preferred_element_type=jnp.float32)


def matmul_tn(left, right):
    return lax.dot_general(
        left, right, (((0,), (0,)), ((), ())), precision=precise, preferred_element_type=jnp.float32
    )


def matmul_nt(left, right):
    return lax.dot_general(
        left, right, (((1,), (1,)), ((), ())), precision=precise, preferred_element_type=jnp.float32
    )


def exchanged(value, axis, distance):
    pairs = [(source, source ^ distance) for source in range(lax.axis_size(axis))]
    return lax.ppermute(value, axis, pairs)


def scattered_sum(value, axis, group):
    place = lax.axis_index(axis) % group
    rows = value.shape[0] // group
    total = lax.dynamic_slice_in_dim(value, place * rows, rows)
    parts = [
        exchanged(lax.dynamic_slice_in_dim(value, (place ^ distance) * rows, rows), axis, distance)
        for distance in range(1, group)
    ]
    for part in parts:
        total = total + part
    return total


def gathered(value, axis, group):
    place = lax.axis_index(axis) % group
    rows = value.shape[0]
    whole = jnp.zeros((group * rows,) + value.shape[1:], value.dtype)
    whole = lax.dynamic_update_slice_in_dim(whole, value, place * rows, 0)
    for distance in range(1, group):
        part = exchanged(value, axis, distance)
        whole = lax.dynamic_update_slice_in_dim(whole, part, (place ^ distance) * rows, 0)
    return whole


def summed(value):
    mode_size, col_size = lax.axis_size("mode"), lax.axis_size("col")
    col_group = min(2, col_size)
    mode_group = min(4, mode_size)
    value = scattered_sum(value, "col", col_group)
    value = scattered_sum(value, "mode", mode_group)
    distance = mode_group
    while distance < mode_size:
        value = value + exchanged(value, "mode", distance)
        distance *= 2
    distance = col_group
    while distance < col_size:
        value = value + exchanged(value, "col", distance)
        distance *= 2
    value = gathered(value, "mode", mode_group)
    return gathered(value, "col", col_group)


def row_of(tile, index):
    return jnp.broadcast_to(tile[index : index + 1, :], tile.shape)


def lane_of(tile, index):
    return jnp.take_along_axis(tile, jnp.full(tile.shape, index, jnp.int32), axis=1)


def factored(block, with_upper):
    side = block.shape[0]
    count = side // SUB
    width = PANEL * SUB
    row = lax.broadcasted_iota(jnp.int32, (SUB, side), 0)
    lane = lax.broadcasted_iota(jnp.int32, (SUB, side), 1)
    tiles = [block[SUB * t : SUB * t + SUB, :] for t in range(count)]
    scales = [None] * count
    members = range(PANEL)
    for first in range(0, count, PANEL):
        base = first * SUB
        inside = (lane >= base) & (lane < base + width)
        columns = [[lane_of(tiles[first + h], base + j) for h in members] for j in range(width)]
        near = range(first + PANEL, min(first + 2 * PANEL, count))
        far = range(first + 2 * PANEL, count)
        below = {t: [lane_of(tiles[t], base + j) for j in range(width)] for t in near}
        panel = [tiles[first + h] for h in members]
        if far:
            sent = jnp.concatenate([jnp.where(lane >= base + width + width, panel[h], 0.0) for h in members])
        kept, scale = list(panel), [None] * PANEL
        for pivot in range(width):
            own, place = divmod(pivot, SUB)
            here = row == place
            cleared = lane == base + pivot
            reciprocal = pl.reciprocal(row_of(columns[pivot][own], place), approx=True)
            scale[own] = jnp.where(here, reciprocal, scale[own]) if place else reciprocal
            kept[own] = jnp.where(here, panel[own], kept[own]) if place else panel[own]
            factor = [
                (jnp.where(here, 0.0, columns[pivot][h]) if h == own else columns[pivot][h]) * reciprocal
                for h in members
            ]
            for j in range(pivot + 1, width):
                value = row_of(columns[j][own], place)
                columns[j] = [columns[j][h] - factor[h] * value for h in members]
            value = jnp.where(cleared, 1.0, row_of(panel[own], place))
            panel = [
                jnp.where(cleared, jnp.where(here, 1.0, 0.0) if h == own else 0.0, panel[h]) - factor[h] * value
                for h in members
            ]
        for h in members:
            tiles[first + h] = kept[h]
            scales[first + h] = scale[h]
        if near:
            reduced = [panel[h] * scale[h] for h in members]
            rows = [row_of(reduced[m // SUB], m % SUB) for m in range(width)]
            for t in near:
                even = jnp.where(inside, 0.0, tiles[t])
                odd = None
                for m in range(width):
                    term = below[t][m] * rows[m]
                    if m % 2:
                        odd = term if odd is None else odd + term
                    else:
                        even = even - term
                tiles[t] = even - odd
            if far:
                update = matmul_tn(sent, jnp.concatenate(reduced))
                for t in far:
                    tiles[t] = jnp.where(inside, 0.0, tiles[t]) - update[SUB * t : SUB * t + SUB]
    uppers, inverses = [], []
    for t in range(count):
        root = lax.rsqrt(scales[t]) * scales[t]
        scaled = tiles[t] * root
        diagonal = row + SUB * t
        uppers.append(jnp.where(lane >= diagonal, scaled, 0.0))
        inverses.append(jnp.where(lane < diagonal, scaled, jnp.where(lane == diagonal, root, 0.0)))
    return (jnp.concatenate(uppers) if with_upper else None), jnp.concatenate(inverses)


def block_places(tiles):
    return {
        pair: place for place, pair in enumerate((i, j) for i in range(tiles) for j in range(i, tiles))
    }


def write_triangle(packed_ref, outbox_ref, tiles):
    places = block_places(tiles)
    blocks = {pair: packed_ref[TILE * at : TILE * at + TILE, :] for pair, at in places.items()}
    for k in range(tiles):
        blocks[k, k], inverse = factored(blocks[k, k], True)
        for j in range(k + 1, tiles):
            blocks[k, j] = matmul(inverse, blocks[k, j])
        for j in range(k, tiles):
            at = places[k, j]
            outbox_ref[TILE * at : TILE * at + TILE, :] = blocks[k, j]
        for i in range(k + 1, tiles):
            for j in range(i, tiles):
                blocks[i, j] = blocks[i, j] - matmul_tn(blocks[k, i], blocks[k, j])


def write_basis(packed_ref, initial_ref, outbox_ref, gram_ref, tiles):
    for (i, j), at in block_places(tiles).items():
        block = packed_ref[TILE * at : TILE * at + TILE, :]
        gram_ref[TILE * i : TILE * i + TILE, TILE * j : TILE * j + TILE] = block
        if i != j:
            gram_ref[TILE * j : TILE * j + TILE, TILE * i : TILE * i + TILE] = block.T
    product_t = matmul(initial_ref[...].T, gram_ref[...])
    for sweep in range(ITERS):
        inner = matmul_nt(product_t, product_t)
        if sweep < ITERS - 1:
            following = matmul(product_t, gram_ref[...])
        _, inverse = factored(inner, False)
        if sweep < ITERS - 1:
            product_t = matmul(inverse, following)
    current_t = matmul(inverse, product_t)
    rows = current_t.shape[1]
    outbox_ref[:rows, :] = current_t.T
    for i in range(tiles):
        outbox_ref[rows + TILE * i : rows + TILE * i + TILE, :] = current_t[:, TILE * i : TILE * i + TILE]


def factor_kernel(tiles, part_ref, packed_ref, initial_ref, outbox_ref, gram_ref):
    @pl.when(part_ref[0] == 0)
    def _():
        write_triangle(packed_ref, outbox_ref, tiles)

    @pl.when(part_ref[0] != 0)
    def _():
        write_basis(packed_ref, initial_ref, outbox_ref, gram_ref, tiles)


def closing_kernel(tiles, part_ref, outbox_ref, inbox_ref, unfold_ref, core_ref, basis_ref, triangle_ref):
    def close(triangle_box, basis_box):
        places = block_places(tiles)
        rows = basis_ref.shape[0]
        current_t = jnp.concatenate(
            [basis_box[rows + TILE * i : rows + TILE * i + TILE, :] for i in range(tiles)], axis=1
        )
        core_flat = matmul(current_t, unfold_ref[...])
        cells = core_ref.shape[2]
        for slab in range(core_ref.shape[1]):
            core_ref[:, slab, :] = core_flat[:, slab * cells : slab * cells + cells]
        basis_ref[...] = basis_box[:rows, :]
        for i in range(tiles):
            for j in range(tiles):
                at = places.get((i, j))
                triangle_ref[TILE * i : TILE * i + TILE, TILE * j : TILE * j + TILE] = (
                    jnp.zeros((TILE, TILE), jnp.float32)
                    if at is None
                    else triangle_box[TILE * at : TILE * at + TILE, :]
                )

    @pl.when(part_ref[0] == 0)
    def _():
        close(outbox_ref, inbox_ref)

    @pl.when(part_ref[0] != 0)
    def _():
        close(inbox_ref, outbox_ref)


VMEM_LIMIT = 32 * 2**20


def factors(packed, initial, part):
    rows, keep = initial.shape
    tiles = rows // TILE
    vmem = pl.BlockSpec(memory_space=pltpu.VMEM)
    return pl.pallas_call(
        functools.partial(factor_kernel, tiles),
        out_shape=jax.ShapeDtypeStruct((max(packed.shape[0], rows + tiles * keep), TILE), jnp.float32),
        in_specs=[pl.BlockSpec(memory_space=pltpu.SMEM), vmem, vmem],
        out_specs=vmem,
        scratch_shapes=[pltpu.VMEM((rows, rows), jnp.float32)],
        compiler_params=pltpu.CompilerParams(vmem_limit_bytes=VMEM_LIMIT),
    )(part, packed, initial)


def finished(packed, initial, unfold, slab_count):
    rows, keep = initial.shape
    if lax.axis_size("col") % 2 == 0:
        part = jnp.full((1,), lax.axis_index("col") % 2, jnp.int32)
        outbox = factors(packed, initial, part)
        inbox = exchanged(outbox, "col", 1)
    else:
        part = jnp.zeros((1,), jnp.int32)
        outbox = factors(packed, initial, part)
        inbox = factors(packed, initial, part + 1)
    vmem = pl.BlockSpec(memory_space=pltpu.VMEM)
    return pl.pallas_call(
        functools.partial(closing_kernel, rows // TILE),
        out_shape=[
            jax.ShapeDtypeStruct((keep, slab_count, unfold.shape[1] // slab_count), jnp.float32),
            jax.ShapeDtypeStruct((rows, keep), jnp.float32),
            jax.ShapeDtypeStruct((rows, rows), jnp.float32),
        ],
        in_specs=[pl.BlockSpec(memory_space=pltpu.SMEM), vmem, vmem, vmem],
        out_specs=[vmem, vmem, vmem],
        compiler_params=pltpu.CompilerParams(vmem_limit_bytes=VMEM_LIMIT),
    )(part, outbox, inbox, unfold)


def blocks_kernel(tensor_ref, blocks_ref):
    count, _, columns = blocks_ref.shape
    slab_count = tensor_ref.shape[1]
    cells = columns // slab_count
    for part in range(count):
        for slab in range(slab_count):
            blocks_ref[part, :, slab * cells : slab * cells + cells] = tensor_ref[
                :, slab, part * cells : part * cells + cells
            ]


def blocks_of(tensor, count):
    rows, slab_count, width = tensor.shape
    vmem = pl.BlockSpec(memory_space=pltpu.VMEM)
    return pl.pallas_call(
        blocks_kernel,
        out_shape=jax.ShapeDtypeStruct((count, rows, slab_count * width // count), jnp.float32),
        in_specs=[vmem],
        out_specs=vmem,
        compiler_params=pltpu.CompilerParams(vmem_limit_bytes=VMEM_LIMIT),
    )(tensor)


def local(tensor, initial):
    mode_size = lax.axis_size("mode")
    row_part, slab_count, width = tensor.shape
    row_count = row_part * mode_size
    column_total = slab_count * width * lax.axis_size("col")
    regrouped = lax.all_to_all(blocks_of(tensor, mode_size), "mode", split_axis=0, concat_axis=0, tiled=True)
    unfold = regrouped.reshape(row_count, slab_count * width // mode_size)
    local_gram = matmul(unfold, unfold.T) / column_total
    packed = jnp.concatenate(
        [
            local_gram[i * TILE : (i + 1) * TILE, j * TILE : (j + 1) * TILE]
            for i, j in block_places(row_count // TILE)
        ]
    )
    return finished(summed(packed), initial, unfold, slab_count)


def solution(mesh):
    return jax.shard_map(
        local,
        mesh=mesh,
        in_specs=(P("mode", "col", None), P()),
        out_specs=(P(None, "col", "mode"), P(), P()),
        check_vma=False,
    )
```

```python
import functools

import jax
import jax.numpy as jnp
from jax import lax
from jax.experimental import pallas as pl
from jax.experimental.pallas import tpu as pltpu
from jax.sharding import PartitionSpec as P

ITERS = 3
TILE = 128
SUB = 8
PANEL = 2

precise = lax.Precision.HIGHEST


def matmul(left, right):
    return jnp.dot(left, right, precision=precise, preferred_element_type=jnp.float32)


def matmul_tn(left, right):
    return lax.dot_general(
        left, right, (((0,), (0,)), ((), ())), precision=precise, preferred_element_type=jnp.float32
    )


def matmul_nt(left, right):
    return lax.dot_general(
        left, right, (((1,), (1,)), ((), ())), precision=precise, preferred_element_type=jnp.float32
    )


def exchanged(value, axis, distance):
    pairs = [(source, source ^ distance) for source in range(lax.axis_size(axis))]
    return lax.ppermute(value, axis, pairs)


def scattered_sum(value, axis, group):
    place = lax.axis_index(axis) % group
    rows = value.shape[0] // group
    total = lax.dynamic_slice_in_dim(value, place * rows, rows)
    parts = [
        exchanged(lax.dynamic_slice_in_dim(value, (place ^ distance) * rows, rows), axis, distance)
        for distance in range(1, group)
    ]
    for part in parts:
        total = total + part
    return total


def gathered(value, axis, group):
    place = lax.axis_index(axis) % group
    rows = value.shape[0]
    whole = jnp.zeros((group * rows,) + value.shape[1:], value.dtype)
    whole = lax.dynamic_update_slice_in_dim(whole, value, place * rows, 0)
    for distance in range(1, group):
        part = exchanged(value, axis, distance)
        whole = lax.dynamic_update_slice_in_dim(whole, part, (place ^ distance) * rows, 0)
    return whole


def summed(value):
    mode_size, col_size = lax.axis_size("mode"), lax.axis_size("col")
    col_group = min(2, col_size)
    mode_group = min(4, mode_size)
    value = scattered_sum(value, "col", col_group)
    value = scattered_sum(value, "mode", mode_group)
    distance = mode_group
    while distance < mode_size:
        value = value + exchanged(value, "mode", distance)
        distance *= 2
    distance = col_group
    while distance < col_size:
        value = value + exchanged(value, "col", distance)
        distance *= 2
    value = gathered(value, "mode", mode_group)
    return gathered(value, "col", col_group)


def row_of(tile, index):
    return jnp.broadcast_to(tile[index : index + 1, :], tile.shape)


def lane_of(tile, index):
    return jnp.take_along_axis(tile, jnp.full(tile.shape, index, jnp.int32), axis=1)


def factored(block, with_upper):
    side = block.shape[0]
    count = side // SUB
    width = PANEL * SUB
    row = lax.broadcasted_iota(jnp.int32, (SUB, side), 0)
    lane = lax.broadcasted_iota(jnp.int32, (SUB, side), 1)
    tiles = [block[SUB * t : SUB * t + SUB, :] for t in range(count)]
    scales = [None] * count
    members = range(PANEL)
    for first in range(0, count, PANEL):
        base = first * SUB
        inside = (lane >= base) & (lane < base + width)
        columns = [[lane_of(tiles[first + h], base + j) for h in members] for j in range(width)]
        near = range(first + PANEL, min(first + 2 * PANEL, count))
        far = range(first + 2 * PANEL, count)
        below = {t: [lane_of(tiles[t], base + j) for j in range(width)] for t in near}
        panel = [tiles[first + h] for h in members]
        if far:
            sent = jnp.concatenate([jnp.where(lane >= base + width + width, panel[h], 0.0) for h in members])
        kept, scale = list(panel), [None] * PANEL
        for pivot in range(width):
            own, place = divmod(pivot, SUB)
            here = row == place
            cleared = lane == base + pivot
            reciprocal = pl.reciprocal(row_of(columns[pivot][own], place), approx=True)
            scale[own] = jnp.where(here, reciprocal, scale[own]) if place else reciprocal
            kept[own] = jnp.where(here, panel[own], kept[own]) if place else panel[own]
            factor = [
                (jnp.where(here, 0.0, columns[pivot][h]) if h == own else columns[pivot][h]) * reciprocal
                for h in members
            ]
            for j in range(pivot + 1, width):
                value = row_of(columns[j][own], place)
                columns[j] = [columns[j][h] - factor[h] * value for h in members]
            value = jnp.where(cleared, 1.0, row_of(panel[own], place))
            panel = [
                jnp.where(cleared, jnp.where(here, 1.0, 0.0) if h == own else 0.0, panel[h]) - factor[h] * value
                for h in members
            ]
        for h in members:
            tiles[first + h] = kept[h]
            scales[first + h] = scale[h]
        if near:
            reduced = [panel[h] * scale[h] for h in members]
            rows = [row_of(reduced[m // SUB], m % SUB) for m in range(width)]
            for t in near:
                even = jnp.where(inside, 0.0, tiles[t])
                odd = None
                for m in range(width):
                    term = below[t][m] * rows[m]
                    if m % 2:
                        odd = term if odd is None else odd + term
                    else:
                        even = even - term
                tiles[t] = even - odd
            if far:
                update = matmul_tn(sent, jnp.concatenate(reduced))
                for t in far:
                    tiles[t] = jnp.where(inside, 0.0, tiles[t]) - update[SUB * t : SUB * t + SUB]
    uppers, inverses = [], []
    for t in range(count):
        root = lax.rsqrt(scales[t]) * scales[t]
        scaled = tiles[t] * root
        diagonal = row + SUB * t
        uppers.append(jnp.where(lane >= diagonal, scaled, 0.0))
        inverses.append(jnp.where(lane < diagonal, scaled, jnp.where(lane == diagonal, root, 0.0)))
    return (jnp.concatenate(uppers) if with_upper else None), jnp.concatenate(inverses)


def block_places(tiles):
    return {
        pair: place for place, pair in enumerate((i, j) for i in range(tiles) for j in range(i, tiles))
    }


def write_triangle(packed_ref, outbox_ref, tiles):
    places = block_places(tiles)
    blocks = {pair: packed_ref[TILE * at : TILE * at + TILE, :] for pair, at in places.items()}
    for k in range(tiles):
        blocks[k, k], inverse = factored(blocks[k, k], True)
        for j in range(k + 1, tiles):
            blocks[k, j] = matmul(inverse, blocks[k, j])
        for j in range(k, tiles):
            at = places[k, j]
            outbox_ref[TILE * at : TILE * at + TILE, :] = blocks[k, j]
        for i in range(k + 1, tiles):
            for j in range(i, tiles):
                blocks[i, j] = blocks[i, j] - matmul_tn(blocks[k, i], blocks[k, j])


def write_basis(packed_ref, initial_ref, outbox_ref, gram_ref, tiles):
    for (i, j), at in block_places(tiles).items():
        block = packed_ref[TILE * at : TILE * at + TILE, :]
        gram_ref[TILE * i : TILE * i + TILE, TILE * j : TILE * j + TILE] = block
        if i != j:
            gram_ref[TILE * j : TILE * j + TILE, TILE * i : TILE * i + TILE] = block.T
    product_t = matmul(initial_ref[...].T, gram_ref[...])
    for sweep in range(ITERS):
        inner = matmul_nt(product_t, product_t)
        if sweep < ITERS - 1:
            following = matmul(product_t, gram_ref[...])
        _, inverse = factored(inner, False)
        if sweep < ITERS - 1:
            product_t = matmul(inverse, following)
    current_t = matmul(inverse, product_t)
    rows = current_t.shape[1]
    outbox_ref[:rows, :] = current_t.T
    for i in range(tiles):
        outbox_ref[rows + TILE * i : rows + TILE * i + TILE, :] = current_t[:, TILE * i : TILE * i + TILE]


def factor_kernel(tiles, part_ref, packed_ref, initial_ref, outbox_ref, gram_ref):
    @pl.when(part_ref[0] == 0)
    def _():
        write_triangle(packed_ref, outbox_ref, tiles)

    @pl.when(part_ref[0] != 0)
    def _():
        write_basis(packed_ref, initial_ref, outbox_ref, gram_ref, tiles)


def closing_kernel(tiles, part_ref, outbox_ref, inbox_ref, *refs):
    *unfold_refs, core_ref, basis_ref, triangle_ref = refs

    def close(triangle_box, basis_box):
        places = block_places(tiles)
        rows = basis_ref.shape[0]
        current_t = jnp.concatenate(
            [basis_box[rows + TILE * i : rows + TILE * i + TILE, :] for i in range(tiles)], axis=1
        )
        slabs = core_ref.shape[1] // len(unfold_refs)
        cells = core_ref.shape[2]
        for half, unfold_ref in enumerate(unfold_refs):
            core_flat = matmul(current_t, unfold_ref[...])
            for slab in range(slabs):
                core_ref[:, half * slabs + slab, :] = core_flat[:, slab * cells : slab * cells + cells]
        basis_ref[...] = basis_box[:rows, :]
        for i in range(tiles):
            for j in range(tiles):
                at = places.get((i, j))
                triangle_ref[TILE * i : TILE * i + TILE, TILE * j : TILE * j + TILE] = (
                    jnp.zeros((TILE, TILE), jnp.float32)
                    if at is None
                    else triangle_box[TILE * at : TILE * at + TILE, :]
                )

    @pl.when(part_ref[0] == 0)
    def _():
        close(outbox_ref, inbox_ref)

    @pl.when(part_ref[0] != 0)
    def _():
        close(inbox_ref, outbox_ref)


VMEM_LIMIT = 32 * 2**20


def factors(packed, initial, part):
    rows, keep = initial.shape
    tiles = rows // TILE
    vmem = pl.BlockSpec(memory_space=pltpu.VMEM)
    return pl.pallas_call(
        functools.partial(factor_kernel, tiles),
        out_shape=jax.ShapeDtypeStruct((max(packed.shape[0], rows + tiles * keep), TILE), jnp.float32),
        in_specs=[pl.BlockSpec(memory_space=pltpu.SMEM), vmem, vmem],
        out_specs=vmem,
        scratch_shapes=[pltpu.VMEM((rows, rows), jnp.float32)],
        compiler_params=pltpu.CompilerParams(vmem_limit_bytes=VMEM_LIMIT),
    )(part, packed, initial)


def finished(packed, initial, unfolds, slab_count):
    rows, keep = initial.shape
    columns = sum(unfold.shape[1] for unfold in unfolds)
    if lax.axis_size("col") % 2 == 0:
        part = jnp.full((1,), lax.axis_index("col") % 2, jnp.int32)
        outbox = factors(packed, initial, part)
        inbox = exchanged(outbox, "col", 1)
    else:
        part = jnp.zeros((1,), jnp.int32)
        outbox = factors(packed, initial, part)
        inbox = factors(packed, initial, part + 1)
    vmem = pl.BlockSpec(memory_space=pltpu.VMEM)
    return pl.pallas_call(
        functools.partial(closing_kernel, rows // TILE),
        out_shape=[
            jax.ShapeDtypeStruct((keep, slab_count, columns // slab_count), jnp.float32),
            jax.ShapeDtypeStruct((rows, keep), jnp.float32),
            jax.ShapeDtypeStruct((rows, rows), jnp.float32),
        ],
        in_specs=[pl.BlockSpec(memory_space=pltpu.SMEM)] + [vmem] * (2 + len(unfolds)),
        out_specs=[vmem, vmem, vmem],
        compiler_params=pltpu.CompilerParams(vmem_limit_bytes=VMEM_LIMIT),
    )(part, outbox, inbox, *unfolds)


def digits_of(size):
    digits, stride = [], 1
    while stride < size:
        extent = min(4, size // stride)
        digits.append((stride, extent))
        stride *= extent
    return digits or [(1, 1)]


def digit(code, stride_extent):
    stride, extent = stride_extent
    return code // stride % extent


def blocks_kernel(layout, me_ref, tensor_ref, *out_refs):
    for (slabs, codes), out_ref in zip(layout, out_refs):
        cells = out_ref.shape[2] // len(slabs)
        for at, code in enumerate(codes):
            start = pl.multiple_of((me_ref[0] ^ code) * cells, cells)
            for place, slab in enumerate(slabs):
                out_ref[at, :, place * cells : place * cells + cells] = tensor_ref[:, slab, pl.ds(start, cells)]


def blocks_of(tensor, layout, cells, me):
    rows = tensor.shape[0]
    vmem = pl.BlockSpec(memory_space=pltpu.VMEM)
    return pl.pallas_call(
        functools.partial(blocks_kernel, layout),
        out_shape=[
            jax.ShapeDtypeStruct((len(codes), rows, len(slabs) * cells), jnp.float32) for slabs, codes in layout
        ],
        in_specs=[pl.BlockSpec(memory_space=pltpu.SMEM), vmem],
        out_specs=[vmem] * len(layout),
        compiler_params=pltpu.CompilerParams(vmem_limit_bytes=VMEM_LIMIT),
    )(me, tensor)


def regrouped(tensor, me):
    size = lax.axis_size("mode")
    slab_count, width = tensor.shape[1:]
    digits = digits_of(size)
    halves = 2 if slab_count % 2 == 0 else 1
    part = slab_count // halves
    orders = [digits, digits[::-1]][:halves]
    layout = [
        (tuple(range(half * part, half * part + part)), tuple(c for c in range(size) if digit(c, order[0]) == value))
        for half, order in enumerate(orders)
        for value in range(order[0][1])
    ]
    blocks = iter(blocks_of(tensor, layout, width // size, me))
    codes_of = iter([codes for _, codes in layout])
    groups = [[(next(blocks), next(codes_of)) for _ in range(order[0][1])] for order in orders]
    for step in range(len(digits)):
        for half in reversed(range(halves)):
            order = orders[half]
            if step:
                pieces = {code: array[at] for array, codes in groups[half] for at, code in enumerate(codes)}
                groups[half] = []
                for value in range(order[step][1]):
                    codes = tuple(c for c in range(size) if digit(c, order[step]) == value)
                    groups[half].append((jnp.stack([pieces[c] for c in codes]), codes))
            groups[half] = [
                (exchanged(array, "mode", value * order[step][0]) if value else array, codes)
                for value, (array, codes) in reversed(list(enumerate(groups[half])))
            ]
    return groups


def gram_kernel(codes_of, scale, me_ref, *refs):
    count = len(codes_of)
    block_refs, before_refs, (unfold_ref, packed_ref, rows_ref) = refs[:count], refs[count:-3], refs[-3:]
    for block_ref, codes in zip(block_refs, codes_of):
        for at, code in enumerate(codes):
            rows_ref[me_ref[0] ^ code] = block_ref[at]
    unfold = rows_ref[...].reshape(unfold_ref.shape)
    unfold_ref[...] = unfold
    tiles = unfold.shape[0] // TILE
    places = block_places(tiles)
    for i in range(tiles):
        products = matmul_nt(unfold[TILE * i : TILE * i + TILE], unfold[TILE * i :])
        for j in range(i, tiles):
            at = places[i, j]
            share = products[:, TILE * (j - i) : TILE * (j - i) + TILE] * scale
            for before_ref in before_refs:
                share = share + before_ref[TILE * at : TILE * at + TILE, :]
            packed_ref[TILE * at : TILE * at + TILE, :] = share


def gram_of(group, before, scale, me):
    arrays = [array for array, _ in group]
    codes_of = [codes for _, codes in group]
    size = sum(len(codes) for codes in codes_of)
    rows, columns = arrays[0].shape[1:]
    blocks = len(block_places(size * rows // TILE))
    vmem = pl.BlockSpec(memory_space=pltpu.VMEM)
    return pl.pallas_call(
        functools.partial(gram_kernel, codes_of, scale),
        out_shape=[
            jax.ShapeDtypeStruct((size * rows, columns), jnp.float32),
            jax.ShapeDtypeStruct((blocks * TILE, TILE), jnp.float32),
        ],
        in_specs=[pl.BlockSpec(memory_space=pltpu.SMEM)] + [vmem] * (len(arrays) + len(before)),
        out_specs=[vmem, vmem],
        scratch_shapes=[pltpu.VMEM((size, rows, columns), jnp.float32)],
        compiler_params=pltpu.CompilerParams(vmem_limit_bytes=VMEM_LIMIT),
        cost_estimate=pl.CostEstimate(
            flops=2 * columns * (size * rows) ** 2, bytes_accessed=8 * size * rows * columns, transcendentals=0
        ),
    )(me, *arrays, *before)


def local(tensor, initial):
    _, slab_count, width = tensor.shape
    column_total = slab_count * width * lax.axis_size("col")
    me = jnp.full((1,), lax.axis_index("mode"), jnp.int32)
    groups = regrouped(tensor, me)
    unfolds, packed = [None] * len(groups), []
    for half in reversed(range(len(groups))):
        unfolds[half], total = gram_of(groups[half], packed, 1.0 / column_total, me)
        packed = [total]
    return finished(summed(packed[0]), initial, unfolds, slab_count)


def solution(mesh):
    return jax.shard_map(
        local,
        mesh=mesh,
        in_specs=(P("mode", "col", None), P()),
        out_specs=(P(None, "col", "mode"), P(), P()),
        check_vma=False,
    )
```

```python
import functools

import jax
import jax.numpy as jnp
from jax import lax
from jax.experimental import pallas as pl
from jax.experimental.pallas import tpu as pltpu
from jax.sharding import PartitionSpec as P

ITERS = 3
TILE = 128
SUB = 8
PANEL = 2

precise = lax.Precision.HIGHEST


def matmul(left, right):
    return jnp.dot(left, right, precision=precise, preferred_element_type=jnp.float32)


def matmul_tn(left, right):
    return lax.dot_general(
        left, right, (((0,), (0,)), ((), ())), precision=precise, preferred_element_type=jnp.float32
    )


def matmul_nt(left, right):
    return lax.dot_general(
        left, right, (((1,), (1,)), ((), ())), precision=precise, preferred_element_type=jnp.float32
    )


def exchanged(value, axis, distance):
    pairs = [(source, source ^ distance) for source in range(lax.axis_size(axis))]
    return lax.ppermute(value, axis, pairs)


def scattered_sum(value, axis, group):
    place = lax.axis_index(axis) % group
    rows = value.shape[0] // group
    total = lax.dynamic_slice_in_dim(value, place * rows, rows)
    parts = [
        exchanged(lax.dynamic_slice_in_dim(value, (place ^ distance) * rows, rows), axis, distance)
        for distance in range(1, group)
    ]
    for part in parts:
        total = total + part
    return total


def gathered(value, axis, group):
    place = lax.axis_index(axis) % group
    rows = value.shape[0]
    whole = jnp.zeros((group * rows,) + value.shape[1:], value.dtype)
    whole = lax.dynamic_update_slice_in_dim(whole, value, place * rows, 0)
    for distance in range(1, group):
        part = exchanged(value, axis, distance)
        whole = lax.dynamic_update_slice_in_dim(whole, part, (place ^ distance) * rows, 0)
    return whole


def summed(share, other_share=None):
    mode_size, col_size = lax.axis_size("mode"), lax.axis_size("col")
    mode_group = min(4, mode_size)
    value = share if other_share is None else share + exchanged(other_share, "col", 1)
    value = scattered_sum(value, "mode", mode_group)
    distance = mode_group
    while distance < mode_size:
        value = value + exchanged(value, "mode", distance)
        distance *= 2
    distance = 1 if other_share is None else 2
    while distance < col_size:
        value = value + exchanged(value, "col", distance)
        distance *= 2
    value = gathered(value, "mode", mode_group)
    return value if other_share is None else gathered(value, "col", 2)


def row_of(tile, index):
    return jnp.broadcast_to(tile[index : index + 1, :], tile.shape)


def lane_of(tile, index):
    return jnp.take_along_axis(tile, jnp.full(tile.shape, index, jnp.int32), axis=1)


def factored(block, with_upper):
    side = block.shape[0]
    count = side // SUB
    width = PANEL * SUB
    row = lax.broadcasted_iota(jnp.int32, (SUB, side), 0)
    lane = lax.broadcasted_iota(jnp.int32, (SUB, side), 1)
    tiles = [block[SUB * t : SUB * t + SUB, :] for t in range(count)]
    scales = [None] * count
    members = range(PANEL)
    for first in range(0, count, PANEL):
        base = first * SUB
        inside = (lane >= base) & (lane < base + width)
        columns = [[lane_of(tiles[first + h], base + j) for h in members] for j in range(width)]
        near = range(first + PANEL, min(first + 2 * PANEL, count))
        far = range(first + 2 * PANEL, count)
        below = {t: [lane_of(tiles[t], base + j) for j in range(width)] for t in near}
        panel = [tiles[first + h] for h in members]
        if far:
            sent = jnp.concatenate([jnp.where(lane >= base + width + width, panel[h], 0.0) for h in members])
        kept, scale = list(panel), [None] * PANEL
        for pivot in range(width):
            own, place = divmod(pivot, SUB)
            here = row == place
            cleared = lane == base + pivot
            reciprocal = pl.reciprocal(row_of(columns[pivot][own], place), approx=True)
            scale[own] = jnp.where(here, reciprocal, scale[own]) if place else reciprocal
            kept[own] = jnp.where(here, panel[own], kept[own]) if place else panel[own]
            factor = [
                (jnp.where(here, 0.0, columns[pivot][h]) if h == own else columns[pivot][h]) * reciprocal
                for h in members
            ]
            for j in range(pivot + 1, width):
                value = row_of(columns[j][own], place)
                columns[j] = [columns[j][h] - factor[h] * value for h in members]
            value = jnp.where(cleared, 1.0, row_of(panel[own], place))
            panel = [
                jnp.where(cleared, jnp.where(here, 1.0, 0.0) if h == own else 0.0, panel[h]) - factor[h] * value
                for h in members
            ]
        for h in members:
            tiles[first + h] = kept[h]
            scales[first + h] = scale[h]
        if near:
            reduced = [panel[h] * scale[h] for h in members]
            rows = [row_of(reduced[m // SUB], m % SUB) for m in range(width)]
            for t in near:
                even = jnp.where(inside, 0.0, tiles[t])
                odd = None
                for m in range(width):
                    term = below[t][m] * rows[m]
                    if m % 2:
                        odd = term if odd is None else odd + term
                    else:
                        even = even - term
                tiles[t] = even - odd
            if far:
                update = matmul_tn(sent, jnp.concatenate(reduced))
                for t in far:
                    tiles[t] = jnp.where(inside, 0.0, tiles[t]) - update[SUB * t : SUB * t + SUB]
    uppers, inverses = [], []
    for t in range(count):
        root = lax.rsqrt(scales[t]) * scales[t]
        scaled = tiles[t] * root
        diagonal = row + SUB * t
        uppers.append(jnp.where(lane >= diagonal, scaled, 0.0))
        inverses.append(jnp.where(lane < diagonal, scaled, jnp.where(lane == diagonal, root, 0.0)))
    return (jnp.concatenate(uppers) if with_upper else None), jnp.concatenate(inverses)


def block_places(tiles):
    return {
        pair: place for place, pair in enumerate((i, j) for i in range(tiles) for j in range(i, tiles))
    }


def write_triangle(packed_ref, outbox_ref, tiles):
    places = block_places(tiles)
    blocks = {pair: packed_ref[TILE * at : TILE * at + TILE, :] for pair, at in places.items()}
    for k in range(tiles):
        blocks[k, k], inverse = factored(blocks[k, k], True)
        for j in range(k + 1, tiles):
            blocks[k, j] = matmul(inverse, blocks[k, j])
        for j in range(k, tiles):
            at = places[k, j]
            outbox_ref[TILE * at : TILE * at + TILE, :] = blocks[k, j]
        for i in range(k + 1, tiles):
            for j in range(i, tiles):
                blocks[i, j] = blocks[i, j] - matmul_tn(blocks[k, i], blocks[k, j])


def write_basis(packed_ref, initial_ref, outbox_ref, gram_ref, tiles):
    for (i, j), at in block_places(tiles).items():
        block = packed_ref[TILE * at : TILE * at + TILE, :]
        gram_ref[TILE * i : TILE * i + TILE, TILE * j : TILE * j + TILE] = block
        if i != j:
            gram_ref[TILE * j : TILE * j + TILE, TILE * i : TILE * i + TILE] = block.T
    product_t = matmul(initial_ref[...].T, gram_ref[...])
    for sweep in range(ITERS):
        inner = matmul_nt(product_t, product_t)
        if sweep < ITERS - 1:
            following = matmul(product_t, gram_ref[...])
        _, inverse = factored(inner, False)
        if sweep < ITERS - 1:
            product_t = matmul(inverse, following)
    current_t = matmul(inverse, product_t)
    rows = current_t.shape[1]
    outbox_ref[:rows, :] = current_t.T
    for i in range(tiles):
        outbox_ref[rows + TILE * i : rows + TILE * i + TILE, :] = current_t[:, TILE * i : TILE * i + TILE]


def factor_kernel(tiles, part_ref, packed_ref, initial_ref, outbox_ref, gram_ref):
    @pl.when(part_ref[0] == 0)
    def _():
        write_triangle(packed_ref, outbox_ref, tiles)

    @pl.when(part_ref[0] != 0)
    def _():
        write_basis(packed_ref, initial_ref, outbox_ref, gram_ref, tiles)


def closing_kernel(
    tiles, part_ref, outbox_ref, inbox_ref, unfold_ref, core_ref, basis_ref, triangle_ref, zero_ref, semaphores
):
    def close(triangle_box, basis_box):
        places = block_places(tiles)
        rows = basis_ref.shape[0]
        copies = [(basis_box.at[pl.ds(0, rows)], basis_ref)]
        for i in range(tiles):
            for j in range(tiles):
                at = places.get((i, j))
                source = zero_ref if at is None else triangle_box.at[pl.ds(TILE * at, TILE)]
                copies.append((source, triangle_ref.at[pl.ds(TILE * i, TILE), pl.ds(TILE * j, TILE)]))
        copies = [
            pltpu.make_async_copy(source, target, semaphores.at[n]) for n, (source, target) in enumerate(copies)
        ]
        for copy in copies:
            copy.start()
        current_t = jnp.concatenate(
            [basis_box[rows + TILE * i : rows + TILE * i + TILE, :] for i in range(tiles)], axis=1
        )
        core_flat = matmul(current_t, unfold_ref[...])
        cells = core_ref.shape[2]
        for slab in range(core_ref.shape[1]):
            core_ref[:, slab, :] = core_flat[:, slab * cells : slab * cells + cells]
        for copy in copies:
            copy.wait()

    zero_ref[...] = jnp.zeros_like(zero_ref)

    @pl.when(part_ref[0] == 0)
    def _():
        close(outbox_ref, inbox_ref)

    @pl.when(part_ref[0] != 0)
    def _():
        close(inbox_ref, outbox_ref)


VMEM_LIMIT = 32 * 2**20


def factors(packed, initial, part):
    rows, keep = initial.shape
    tiles = rows // TILE
    vmem = pl.BlockSpec(memory_space=pltpu.VMEM)
    return pl.pallas_call(
        functools.partial(factor_kernel, tiles),
        out_shape=jax.ShapeDtypeStruct((max(packed.shape[0], rows + tiles * keep), TILE), jnp.float32),
        in_specs=[pl.BlockSpec(memory_space=pltpu.SMEM), vmem, vmem],
        out_specs=vmem,
        scratch_shapes=[pltpu.VMEM((rows, rows), jnp.float32)],
        compiler_params=pltpu.CompilerParams(vmem_limit_bytes=VMEM_LIMIT),
    )(part, packed, initial)


def finished(packed, initial, unfold, slab_count):
    rows, keep = initial.shape
    if lax.axis_size("col") % 2 == 0:
        part = jnp.full((1,), lax.axis_index("col") % 2, jnp.int32)
        outbox = factors(packed, initial, part)
        inbox = exchanged(outbox, "col", 1)
    else:
        part = jnp.zeros((1,), jnp.int32)
        outbox = factors(packed, initial, part)
        inbox = factors(packed, initial, part + 1)
    vmem = pl.BlockSpec(memory_space=pltpu.VMEM)
    return pl.pallas_call(
        functools.partial(closing_kernel, rows // TILE),
        out_shape=[
            jax.ShapeDtypeStruct((keep, slab_count, unfold.shape[1] // slab_count), jnp.float32),
            jax.ShapeDtypeStruct((rows, keep), jnp.float32),
            jax.ShapeDtypeStruct((rows, rows), jnp.float32),
        ],
        in_specs=[pl.BlockSpec(memory_space=pltpu.SMEM), vmem, vmem, vmem],
        out_specs=[vmem, pl.BlockSpec(memory_space=pl.ANY), pl.BlockSpec(memory_space=pl.ANY)],
        scratch_shapes=[
            pltpu.VMEM((TILE, TILE), jnp.float32),
            pltpu.SemaphoreType.DMA((1 + (rows // TILE) ** 2,)),
        ],
        compiler_params=pltpu.CompilerParams(vmem_limit_bytes=VMEM_LIMIT),
    )(part, outbox, inbox, unfold)


def blocks_kernel(tensor_ref, blocks_ref):
    count, _, columns = blocks_ref.shape
    slab_count = tensor_ref.shape[1]
    cells = columns // slab_count
    for part in range(count):
        for slab in range(slab_count):
            blocks_ref[part, :, slab * cells : slab * cells + cells] = tensor_ref[
                :, slab, part * cells : part * cells + cells
            ]


def blocks_of(tensor, count):
    rows, slab_count, width = tensor.shape
    vmem = pl.BlockSpec(memory_space=pltpu.VMEM)
    return pl.pallas_call(
        blocks_kernel,
        out_shape=jax.ShapeDtypeStruct((count, rows, slab_count * width // count), jnp.float32),
        in_specs=[vmem],
        out_specs=vmem,
        compiler_params=pltpu.CompilerParams(vmem_limit_bytes=VMEM_LIMIT),
    )(tensor)


def gram_kernel(halves, scale, half_ref, unfold_ref, blocks_ref):
    for half, pairs in enumerate(halves):

        @pl.when(half_ref[0] == half)
        def _(pairs=pairs):
            at = 0
            for i in sorted({i for i, _ in pairs}):
                columns = [j for first, j in pairs if first == i]
                left = unfold_ref[TILE * i : TILE * i + TILE, :]
                products = matmul_nt(left, unfold_ref[TILE * columns[0] : TILE * columns[-1] + TILE, :]) * scale
                for n in range(len(columns)):
                    blocks_ref[TILE * at : TILE * at + TILE, :] = products[:, TILE * n : TILE * n + TILE]
                    at += 1


def gram_blocks(unfold, scale, half, halves):
    rows, columns = unfold.shape
    pairs = list(block_places(rows // TILE))
    each = len(pairs) // halves
    parts = [pairs[each * n : each * n + each] for n in range(halves)]
    vmem = pl.BlockSpec(memory_space=pltpu.VMEM)
    return pl.pallas_call(
        functools.partial(gram_kernel, parts, scale),
        out_shape=jax.ShapeDtypeStruct((each * TILE, TILE), jnp.float32),
        in_specs=[pl.BlockSpec(memory_space=pltpu.SMEM), vmem],
        out_specs=vmem,
        compiler_params=pltpu.CompilerParams(vmem_limit_bytes=VMEM_LIMIT),
        cost_estimate=pl.CostEstimate(
            flops=2 * each * TILE * TILE * columns, bytes_accessed=4 * rows * columns, transcendentals=0
        ),
    )(jnp.full((1,), half, jnp.int32), unfold)


def local(tensor, initial):
    mode_size = lax.axis_size("mode")
    row_part, slab_count, width = tensor.shape
    row_count = row_part * mode_size
    column_total = slab_count * width * lax.axis_size("col")
    regrouped = lax.all_to_all(blocks_of(tensor, mode_size), "mode", split_axis=0, concat_axis=0, tiled=True)
    unfold = regrouped.reshape(row_count, slab_count * width // mode_size)
    scale = 1.0 / column_total
    if lax.axis_size("col") % 2 or len(block_places(row_count // TILE)) % 2:
        packed = summed(gram_blocks(unfold, scale, jnp.int32(0), 1))
    else:
        half = lax.axis_index("col") % 2
        other = gram_blocks(unfold, scale, 1 - half, 2)
        packed = summed(gram_blocks(unfold, scale, half, 2), other)
    return finished(packed, initial, unfold, slab_count)


def solution(mesh):
    return jax.shard_map(
        local,
        mesh=mesh,
        in_specs=(P("mode", "col", None), P()),
        out_specs=(P(None, "col", "mode"), P(), P()),
        check_vma=False,
    )
```

```python
import functools

import jax
import jax.numpy as jnp
from jax import lax
from jax.experimental import pallas as pl
from jax.experimental.pallas import tpu as pltpu
from jax.sharding import PartitionSpec as P

ITERS = 3
TILE = 128
SUB = 8
PANEL = 2

precise = lax.Precision.HIGHEST


def matmul(left, right):
    return jnp.dot(left, right, precision=precise, preferred_element_type=jnp.float32)


def matmul_tn(left, right):
    return lax.dot_general(
        left, right, (((0,), (0,)), ((), ())), precision=precise, preferred_element_type=jnp.float32
    )


def matmul_nt(left, right):
    return lax.dot_general(
        left, right, (((1,), (1,)), ((), ())), precision=precise, preferred_element_type=jnp.float32
    )


def exchanged(value, axis, distance):
    pairs = [(source, source ^ distance) for source in range(lax.axis_size(axis))]
    return lax.ppermute(value, axis, pairs)


def scattered_sum(value, axis, group):
    place = lax.axis_index(axis) % group
    rows = value.shape[0] // group
    total = lax.dynamic_slice_in_dim(value, place * rows, rows)
    parts = [
        exchanged(lax.dynamic_slice_in_dim(value, (place ^ distance) * rows, rows), axis, distance)
        for distance in range(1, group)
    ]
    for part in parts:
        total = total + part
    return total


def gathered(value, axis, group):
    place = lax.axis_index(axis) % group
    rows = value.shape[0]
    whole = jnp.zeros((group * rows,) + value.shape[1:], value.dtype)
    whole = lax.dynamic_update_slice_in_dim(whole, value, place * rows, 0)
    for distance in range(1, group):
        part = exchanged(value, axis, distance)
        whole = lax.dynamic_update_slice_in_dim(whole, part, (place ^ distance) * rows, 0)
    return whole


def summed(share, other_share=None):
    mode_size, col_size = lax.axis_size("mode"), lax.axis_size("col")
    mode_group = min(4, mode_size)
    value = share if other_share is None else share + exchanged(other_share, "col", 1)
    value = scattered_sum(value, "mode", mode_group)
    distance = mode_group
    while distance < mode_size:
        value = value + exchanged(value, "mode", distance)
        distance *= 2
    distance = 1 if other_share is None else 2
    while distance < col_size:
        value = value + exchanged(value, "col", distance)
        distance *= 2
    value = gathered(value, "mode", mode_group)
    return value if other_share is None else gathered(value, "col", 2)


def row_of(tile, index):
    return jnp.broadcast_to(tile[index : index + 1, :], tile.shape)


def lane_of(tile, index):
    return jnp.take_along_axis(tile, jnp.full(tile.shape, index, jnp.int32), axis=1)


def factored(block, with_upper):
    side = block.shape[0]
    count = side // SUB
    width = PANEL * SUB
    row = lax.broadcasted_iota(jnp.int32, (SUB, side), 0)
    lane = lax.broadcasted_iota(jnp.int32, (SUB, side), 1)
    tiles = [block[SUB * t : SUB * t + SUB, :] for t in range(count)]
    scales = [None] * count
    members = range(PANEL)
    for first in range(0, count, PANEL):
        base = first * SUB
        inside = (lane >= base) & (lane < base + width)
        columns = [[lane_of(tiles[first + h], base + j) for h in members] for j in range(width)]
        near = range(first + PANEL, min(first + 2 * PANEL, count))
        far = range(first + 2 * PANEL, count)
        below = {t: [lane_of(tiles[t], base + j) for j in range(width)] for t in near}
        panel = [tiles[first + h] for h in members]
        if far:
            sent = jnp.concatenate([jnp.where(lane >= base + width + width, panel[h], 0.0) for h in members])
        kept, scale = list(panel), [None] * PANEL
        for pivot in range(0, width, 2):
            own, place = divmod(pivot, SUB)
            reached = range(own, PANEL)
            here, next_row = row == place, row == place + 1
            at, next_at = lane == base + pivot, lane == base + pivot + 1
            left, right = columns[pivot], columns[pivot + 1]
            a, b = row_of(left[own], place), row_of(right[own], place)
            c = row_of(right[own], place + 1)
            over_a = pl.reciprocal(a, approx=True)
            over_det = pl.reciprocal(a * c - b * b, approx=True)
            left = {h: left[h] for h in reached}
            right = {h: right[h] for h in reached}
            left[own] = jnp.where(here, -1.0, jnp.where(next_row, 0.0, left[own]))
            right[own] = jnp.where(here, 0.0, jnp.where(next_row, -1.0, right[own]))
            factor = {h: (c * left[h] - b * right[h]) * over_det for h in reached}
            next_factor = {h: (a * right[h] - b * left[h]) * over_det for h in reached}

            def reduced_by(value, top, bottom, h):
                return value - factor[h] * top - next_factor[h] * bottom

            for j in range(pivot + 2, width):
                top, bottom = row_of(columns[j][own], place), row_of(columns[j][own], place + 1)
                for h in reached:
                    value = jnp.where(here | next_row, 0.0, columns[j][h]) if h == own else columns[j][h]
                    columns[j][h] = reduced_by(value, top, bottom, h)
            top, bottom = row_of(panel[own], place), row_of(panel[own], place + 1)
            following = jnp.where(at, 0.0, bottom) - (b * over_a) * jnp.where(at, 1.0, top)
            kept[own] = jnp.where(here, panel[own], jnp.where(next_row, following, kept[own]))
            scale[own] = jnp.where(here, over_a, jnp.where(next_row, a * over_det, scale[own] if place else 0.0))
            top = jnp.where(at, 1.0, jnp.where(next_at, 0.0, top))
            bottom = jnp.where(at, 0.0, jnp.where(next_at, 1.0, bottom))
            for h in reached:
                cleared = at | next_at
                if h == own:
                    cleared = cleared | here | next_row
                panel[h] = reduced_by(jnp.where(cleared, 0.0, panel[h]), top, bottom, h)
        for h in reversed(members):
            for later in range(h + 1, PANEL):
                start = base + SUB * later
                panel[h] = jnp.where((lane >= start) & (lane < start + SUB), 0.0, panel[h])
                for m in range(SUB):
                    panel[h] = panel[h] - columns[SUB * later + m][h] * row_of(panel[later], m)
        for h in members:
            tiles[first + h] = kept[h]
            scales[first + h] = scale[h]
        if near:
            reduced = panel
            rows = [row_of(reduced[m // SUB], m % SUB) for m in range(width)]
            for t in near:
                even = jnp.where(inside, 0.0, tiles[t])
                odd = None
                for m in range(width):
                    term = below[t][m] * rows[m]
                    if m % 2:
                        odd = term if odd is None else odd + term
                    else:
                        even = even - term
                tiles[t] = even - odd
            if far:
                update = matmul_tn(sent, jnp.concatenate(reduced))
                for t in far:
                    tiles[t] = jnp.where(inside, 0.0, tiles[t]) - update[SUB * t : SUB * t + SUB]
    uppers, inverses = [], []
    for t in range(count):
        root = lax.rsqrt(scales[t]) * scales[t]
        scaled = tiles[t] * root
        diagonal = row + SUB * t
        uppers.append(jnp.where(lane >= diagonal, scaled, 0.0))
        inverses.append(jnp.where(lane < diagonal, scaled, jnp.where(lane == diagonal, root, 0.0)))
    return (jnp.concatenate(uppers) if with_upper else None), jnp.concatenate(inverses)


def block_places(tiles):
    return {
        pair: place for place, pair in enumerate((i, j) for i in range(tiles) for j in range(i, tiles))
    }


def write_triangle(packed_ref, outbox_ref, tiles):
    places = block_places(tiles)
    blocks = {pair: packed_ref[TILE * at : TILE * at + TILE, :] for pair, at in places.items()}
    for k in range(tiles):
        blocks[k, k], inverse = factored(blocks[k, k], True)
        for j in range(k + 1, tiles):
            blocks[k, j] = matmul(inverse, blocks[k, j])
        for j in range(k, tiles):
            at = places[k, j]
            outbox_ref[TILE * at : TILE * at + TILE, :] = blocks[k, j]
        for i in range(k + 1, tiles):
            for j in range(i, tiles):
                blocks[i, j] = blocks[i, j] - matmul_tn(blocks[k, i], blocks[k, j])


def write_basis(packed_ref, initial_ref, outbox_ref, gram_ref, tiles):
    for (i, j), at in block_places(tiles).items():
        block = packed_ref[TILE * at : TILE * at + TILE, :]
        gram_ref[TILE * i : TILE * i + TILE, TILE * j : TILE * j + TILE] = block
        if i != j:
            gram_ref[TILE * j : TILE * j + TILE, TILE * i : TILE * i + TILE] = block.T
    product_t = matmul(initial_ref[...].T, gram_ref[...])
    for sweep in range(ITERS):
        inner = matmul_nt(product_t, product_t)
        if sweep < ITERS - 1:
            following = matmul(product_t, gram_ref[...])
        _, inverse = factored(inner, False)
        if sweep < ITERS - 1:
            product_t = matmul(inverse, following)
    current_t = matmul(inverse, product_t)
    rows = current_t.shape[1]
    outbox_ref[:rows, :] = current_t.T
    for i in range(tiles):
        outbox_ref[rows + TILE * i : rows + TILE * i + TILE, :] = current_t[:, TILE * i : TILE * i + TILE]


def factor_kernel(tiles, part_ref, packed_ref, initial_ref, outbox_ref, gram_ref):
    @pl.when(part_ref[0] == 0)
    def _():
        write_triangle(packed_ref, outbox_ref, tiles)

    @pl.when(part_ref[0] != 0)
    def _():
        write_basis(packed_ref, initial_ref, outbox_ref, gram_ref, tiles)


def closing_kernel(
    tiles, part_ref, outbox_ref, inbox_ref, unfold_ref, core_ref, basis_ref, triangle_ref, zero_ref, semaphores
):
    def close(triangle_box, basis_box):
        places = block_places(tiles)
        rows = basis_ref.shape[0]
        copies = [(basis_box.at[pl.ds(0, rows)], basis_ref)]
        for i in range(tiles):
            for j in range(tiles):
                at = places.get((i, j))
                source = zero_ref if at is None else triangle_box.at[pl.ds(TILE * at, TILE)]
                copies.append((source, triangle_ref.at[pl.ds(TILE * i, TILE), pl.ds(TILE * j, TILE)]))
        copies = [
            pltpu.make_async_copy(source, target, semaphores.at[n]) for n, (source, target) in enumerate(copies)
        ]
        for copy in copies:
            copy.start()
        current_t = jnp.concatenate(
            [basis_box[rows + TILE * i : rows + TILE * i + TILE, :] for i in range(tiles)], axis=1
        )
        core_flat = matmul(current_t, unfold_ref[...])
        cells = core_ref.shape[2]
        for slab in range(core_ref.shape[1]):
            core_ref[:, slab, :] = core_flat[:, slab * cells : slab * cells + cells]
        for copy in copies:
            copy.wait()

    zero_ref[...] = jnp.zeros_like(zero_ref)

    @pl.when(part_ref[0] == 0)
    def _():
        close(outbox_ref, inbox_ref)

    @pl.when(part_ref[0] != 0)
    def _():
        close(inbox_ref, outbox_ref)


VMEM_LIMIT = 32 * 2**20


def factors(packed, initial, part):
    rows, keep = initial.shape
    tiles = rows // TILE
    vmem = pl.BlockSpec(memory_space=pltpu.VMEM)
    return pl.pallas_call(
        functools.partial(factor_kernel, tiles),
        out_shape=jax.ShapeDtypeStruct((max(packed.shape[0], rows + tiles * keep), TILE), jnp.float32),
        in_specs=[pl.BlockSpec(memory_space=pltpu.SMEM), vmem, vmem],
        out_specs=vmem,
        scratch_shapes=[pltpu.VMEM((rows, rows), jnp.float32)],
        compiler_params=pltpu.CompilerParams(vmem_limit_bytes=VMEM_LIMIT),
    )(part, packed, initial)


def finished(packed, initial, unfold, slab_count):
    rows, keep = initial.shape
    if lax.axis_size("col") % 2 == 0:
        part = jnp.full((1,), lax.axis_index("col") % 2, jnp.int32)
        outbox = factors(packed, initial, part)
        inbox = exchanged(outbox, "col", 1)
    else:
        part = jnp.zeros((1,), jnp.int32)
        outbox = factors(packed, initial, part)
        inbox = factors(packed, initial, part + 1)
    vmem = pl.BlockSpec(memory_space=pltpu.VMEM)
    return pl.pallas_call(
        functools.partial(closing_kernel, rows // TILE),
        out_shape=[
            jax.ShapeDtypeStruct((keep, slab_count, unfold.shape[1] // slab_count), jnp.float32),
            jax.ShapeDtypeStruct((rows, keep), jnp.float32),
            jax.ShapeDtypeStruct((rows, rows), jnp.float32),
        ],
        in_specs=[pl.BlockSpec(memory_space=pltpu.SMEM), vmem, vmem, vmem],
        out_specs=[vmem, pl.BlockSpec(memory_space=pl.ANY), pl.BlockSpec(memory_space=pl.ANY)],
        scratch_shapes=[
            pltpu.VMEM((TILE, TILE), jnp.float32),
            pltpu.SemaphoreType.DMA((1 + (rows // TILE) ** 2,)),
        ],
        compiler_params=pltpu.CompilerParams(vmem_limit_bytes=VMEM_LIMIT),
    )(part, outbox, inbox, unfold)


def blocks_kernel(tensor_ref, blocks_ref):
    count, _, columns = blocks_ref.shape
    slab_count = tensor_ref.shape[1]
    cells = columns // slab_count
    for part in range(count):
        for slab in range(slab_count):
            blocks_ref[part, :, slab * cells : slab * cells + cells] = tensor_ref[
                :, slab, part * cells : part * cells + cells
            ]


def blocks_of(tensor, count):
    rows, slab_count, width = tensor.shape
    vmem = pl.BlockSpec(memory_space=pltpu.VMEM)
    return pl.pallas_call(
        blocks_kernel,
        out_shape=jax.ShapeDtypeStruct((count, rows, slab_count * width // count), jnp.float32),
        in_specs=[vmem],
        out_specs=vmem,
        compiler_params=pltpu.CompilerParams(vmem_limit_bytes=VMEM_LIMIT),
    )(tensor)


def gram_kernel(halves, scale, half_ref, unfold_ref, blocks_ref):
    for half, pairs in enumerate(halves):

        @pl.when(half_ref[0] == half)
        def _(pairs=pairs):
            at = 0
            for i in sorted({i for i, _ in pairs}):
                columns = [j for first, j in pairs if first == i]
                left = unfold_ref[TILE * i : TILE * i + TILE, :]
                products = matmul_nt(left, unfold_ref[TILE * columns[0] : TILE * columns[-1] + TILE, :]) * scale
                for n in range(len(columns)):
                    blocks_ref[TILE * at : TILE * at + TILE, :] = products[:, TILE * n : TILE * n + TILE]
                    at += 1


def gram_blocks(unfold, scale, half, halves):
    rows, columns = unfold.shape
    pairs = list(block_places(rows // TILE))
    each = len(pairs) // halves
    parts = [pairs[each * n : each * n + each] for n in range(halves)]
    vmem = pl.BlockSpec(memory_space=pltpu.VMEM)
    return pl.pallas_call(
        functools.partial(gram_kernel, parts, scale),
        out_shape=jax.ShapeDtypeStruct((each * TILE, TILE), jnp.float32),
        in_specs=[pl.BlockSpec(memory_space=pltpu.SMEM), vmem],
        out_specs=vmem,
        compiler_params=pltpu.CompilerParams(vmem_limit_bytes=VMEM_LIMIT),
        cost_estimate=pl.CostEstimate(
            flops=2 * each * TILE * TILE * columns, bytes_accessed=4 * rows * columns, transcendentals=0
        ),
    )(jnp.full((1,), half, jnp.int32), unfold)


def local(tensor, initial):
    mode_size = lax.axis_size("mode")
    row_part, slab_count, width = tensor.shape
    row_count = row_part * mode_size
    column_total = slab_count * width * lax.axis_size("col")
    regrouped = lax.all_to_all(blocks_of(tensor, mode_size), "mode", split_axis=0, concat_axis=0, tiled=True)
    unfold = regrouped.reshape(row_count, slab_count * width // mode_size)
    scale = 1.0 / column_total
    if lax.axis_size("col") % 2 or len(block_places(row_count // TILE)) % 2:
        packed = summed(gram_blocks(unfold, scale, jnp.int32(0), 1))
    else:
        half = lax.axis_index("col") % 2
        other = gram_blocks(unfold, scale, 1 - half, 2)
        packed = summed(gram_blocks(unfold, scale, half, 2), other)
    return finished(packed, initial, unfold, slab_count)


def solution(mesh):
    return jax.shard_map(
        local,
        mesh=mesh,
        in_specs=(P("mode", "col", None), P()),
        out_specs=(P(None, "col", "mode"), P(), P()),
        check_vma=False,
    )
```

```python
import functools

import jax
import jax.numpy as jnp
from jax import lax
from jax.experimental import pallas as pl
from jax.experimental.pallas import tpu as pltpu
from jax.sharding import PartitionSpec as P

ITERS = 3
TILE = 128
SUB = 8
SPARE = 32
PANEL = 2

precise = lax.Precision.HIGHEST


def matmul(left, right):
    return jnp.dot(left, right, precision=precise, preferred_element_type=jnp.float32)


def matmul_tn(left, right):
    return lax.dot_general(
        left, right, (((0,), (0,)), ((), ())), precision=precise, preferred_element_type=jnp.float32
    )


def matmul_nt(left, right):
    return lax.dot_general(
        left, right, (((1,), (1,)), ((), ())), precision=precise, preferred_element_type=jnp.float32
    )


def exchanged(value, axis, distance):
    pairs = [(source, source ^ distance) for source in range(lax.axis_size(axis))]
    return lax.ppermute(value, axis, pairs)


def scattered_sum(value, axis, group):
    place = lax.axis_index(axis) % group
    rows = value.shape[0] // group
    total = lax.dynamic_slice_in_dim(value, place * rows, rows)
    parts = [
        exchanged(lax.dynamic_slice_in_dim(value, (place ^ distance) * rows, rows), axis, distance)
        for distance in range(1, group)
    ]
    for part in parts:
        total = total + part
    return total


def gathered(value, axis, group):
    place = lax.axis_index(axis) % group
    rows = value.shape[0]
    whole = jnp.zeros((group * rows,) + value.shape[1:], value.dtype)
    whole = lax.dynamic_update_slice_in_dim(whole, value, place * rows, 0)
    for distance in range(1, group):
        part = exchanged(value, axis, distance)
        whole = lax.dynamic_update_slice_in_dim(whole, part, (place ^ distance) * rows, 0)
    return whole


def summed(share, other_share=None):
    mode_size, col_size = lax.axis_size("mode"), lax.axis_size("col")
    mode_group = min(4, mode_size)
    value = share if other_share is None else share + exchanged(other_share, "col", 1)
    value = scattered_sum(value, "mode", mode_group)
    distance = mode_group
    while distance < mode_size:
        value = value + exchanged(value, "mode", distance)
        distance *= 2
    distance = 1 if other_share is None else 2
    while distance < col_size:
        value = value + exchanged(value, "col", distance)
        distance *= 2
    value = gathered(value, "mode", mode_group)
    return value if other_share is None else gathered(value, "col", 2)


def row_of(tile, index):
    return jnp.broadcast_to(tile[index : index + 1, :], tile.shape)


def lane_of(tile, index):
    return jnp.take_along_axis(tile, jnp.full(tile.shape, index, jnp.int32), axis=1)


def factored(block, with_upper):
    side = block.shape[0]
    count = side // SUB
    width = PANEL * SUB
    row = lax.broadcasted_iota(jnp.int32, (SUB, side), 0)
    lane = lax.broadcasted_iota(jnp.int32, (SUB, side), 1)
    tiles = [block[SUB * t : SUB * t + SUB, :] for t in range(count)]
    scales = [None] * count
    members = range(PANEL)
    for first in range(0, count, PANEL):
        base = first * SUB
        inside = (lane >= base) & (lane < base + width)
        columns = [[lane_of(tiles[first + h], base + j) for h in members] for j in range(width)]
        near = range(first + PANEL, min(first + 2 * PANEL, count))
        far = range(first + 2 * PANEL, count)
        below = {t: [lane_of(tiles[t], base + j) for j in range(width)] for t in near}
        panel = [tiles[first + h] for h in members]
        if far:
            sent = jnp.concatenate([jnp.where(lane >= base + width + width, panel[h], 0.0) for h in members])
        kept, scale = list(panel), [None] * PANEL
        for pivot in range(0, width, 2):
            own, place = divmod(pivot, SUB)
            reached = range(own, PANEL)
            here, next_row = row == place, row == place + 1
            at, next_at = lane == base + pivot, lane == base + pivot + 1
            left, right = columns[pivot], columns[pivot + 1]
            a, b = row_of(left[own], place), row_of(right[own], place)
            c = row_of(right[own], place + 1)
            over_a = pl.reciprocal(a, approx=True)
            over_det = pl.reciprocal(a * c - b * b, approx=True)
            left = {h: left[h] for h in reached}
            right = {h: right[h] for h in reached}
            left[own] = jnp.where(here, -1.0, jnp.where(next_row, 0.0, left[own]))
            right[own] = jnp.where(here, 0.0, jnp.where(next_row, -1.0, right[own]))
            factor = {h: (c * left[h] - b * right[h]) * over_det for h in reached}
            next_factor = {h: (a * right[h] - b * left[h]) * over_det for h in reached}

            def reduced_by(value, top, bottom, h):
                return value - factor[h] * top - next_factor[h] * bottom

            for j in range(pivot + 2, width):
                top, bottom = row_of(columns[j][own], place), row_of(columns[j][own], place + 1)
                for h in reached:
                    value = jnp.where(here | next_row, 0.0, columns[j][h]) if h == own else columns[j][h]
                    columns[j][h] = reduced_by(value, top, bottom, h)
            top, bottom = row_of(panel[own], place), row_of(panel[own], place + 1)
            following = jnp.where(at, 0.0, bottom) - (b * over_a) * jnp.where(at, 1.0, top)
            kept[own] = jnp.where(here, panel[own], jnp.where(next_row, following, kept[own]))
            scale[own] = jnp.where(here, over_a, jnp.where(next_row, a * over_det, scale[own] if place else 0.0))
            top = jnp.where(at, 1.0, jnp.where(next_at, 0.0, top))
            bottom = jnp.where(at, 0.0, jnp.where(next_at, 1.0, bottom))
            for h in reached:
                cleared = at | next_at
                if h == own:
                    cleared = cleared | here | next_row
                panel[h] = reduced_by(jnp.where(cleared, 0.0, panel[h]), top, bottom, h)
        for h in reversed(members):
            for later in range(h + 1, PANEL):
                start = base + SUB * later
                panel[h] = jnp.where((lane >= start) & (lane < start + SUB), 0.0, panel[h])
                for m in range(SUB):
                    panel[h] = panel[h] - columns[SUB * later + m][h] * row_of(panel[later], m)
        for h in members:
            tiles[first + h] = kept[h]
            scales[first + h] = scale[h]
        if near:
            reduced = panel
            rows = [row_of(reduced[m // SUB], m % SUB) for m in range(width)]
            for t in near:
                even = jnp.where(inside, 0.0, tiles[t])
                odd = None
                for m in range(width):
                    term = below[t][m] * rows[m]
                    if m % 2:
                        odd = term if odd is None else odd + term
                    else:
                        even = even - term
                tiles[t] = even - odd
            if far:
                update = matmul_tn(sent, jnp.concatenate(reduced))
                for t in far:
                    tiles[t] = jnp.where(inside, 0.0, tiles[t]) - update[SUB * t : SUB * t + SUB]
    uppers, inverses = [], []
    for t in range(count):
        root = lax.rsqrt(scales[t]) * scales[t]
        scaled = tiles[t] * root
        diagonal = row + SUB * t
        uppers.append(jnp.where(lane >= diagonal, scaled, 0.0))
        inverses.append(jnp.where(lane < diagonal, scaled, jnp.where(lane == diagonal, root, 0.0)))
    return (jnp.concatenate(uppers) if with_upper else None), jnp.concatenate(inverses)


def block_places(tiles):
    return {
        pair: place for place, pair in enumerate((i, j) for i in range(tiles) for j in range(i, tiles))
    }


def packing(tiles):
    above = [(i, j) for i in range(tiles) for j in range(i + 1, tiles)]
    doubles = [(i, i + 1) for i in range(0, tiles, 2)]
    cut = len(doubles) // 2
    each = (len(above) + len(doubles)) // 2
    length = each * TILE + SPARE
    halves = []
    for half in range(2):
        base = half * length
        pairs = doubles[cut:] if half else doubles[:cut]
        blocks = above[each - cut :] if half else above[: each - cut]
        places = {pair: (base + TILE * n, base + each * TILE + n) for n, pair in enumerate(pairs)}
        offsets = {pair: base + TILE * (len(pairs) + n) for n, pair in enumerate(blocks)}
        halves.append((offsets, places, base))
    return halves, length


def unpacked(packed_ref, tiles):
    row = lax.broadcasted_iota(jnp.int32, (TILE, TILE), 0)
    lane = lax.broadcasted_iota(jnp.int32, (TILE, TILE), 1)
    blocks = {}
    for offsets, doubles, _ in packing(tiles)[0]:
        for pair, at in offsets.items():
            blocks[pair] = packed_ref[at : at + TILE, :]
        for (i, j), (at, line) in doubles.items():
            both = packed_ref[at : at + TILE, :]
            turned = both.T
            diagonal = jnp.broadcast_to(packed_ref[line : line + 1, :], (TILE, TILE))
            blocks[i, i] = jnp.where(lane >= row, both, turned)
            blocks[j, j] = jnp.where(lane < row, both, jnp.where(lane > row, turned, diagonal))
    return blocks


def write_triangle(packed_ref, outbox_ref, tiles):
    places = block_places(tiles)
    blocks = unpacked(packed_ref, tiles)
    for k in range(tiles):
        blocks[k, k], inverse = factored(blocks[k, k], True)
        for j in range(k + 1, tiles):
            blocks[k, j] = matmul(inverse, blocks[k, j])
        for j in range(k, tiles):
            at = places[k, j]
            outbox_ref[TILE * at : TILE * at + TILE, :] = blocks[k, j]
        for i in range(k + 1, tiles):
            for j in range(i, tiles):
                blocks[i, j] = blocks[i, j] - matmul_tn(blocks[k, i], blocks[k, j])


def write_basis(packed_ref, initial_ref, outbox_ref, gram_ref, tiles):
    for (i, j), block in unpacked(packed_ref, tiles).items():
        gram_ref[TILE * i : TILE * i + TILE, TILE * j : TILE * j + TILE] = block
        if i != j:
            gram_ref[TILE * j : TILE * j + TILE, TILE * i : TILE * i + TILE] = block.T
    product_t = matmul(initial_ref[...].T, gram_ref[...])
    for sweep in range(ITERS):
        inner = matmul_nt(product_t, product_t)
        if sweep < ITERS - 1:
            following = matmul(product_t, gram_ref[...])
        _, inverse = factored(inner, False)
        if sweep < ITERS - 1:
            product_t = matmul(inverse, following)
    current_t = matmul(inverse, product_t)
    rows = current_t.shape[1]
    outbox_ref[:rows, :] = current_t.T
    for i in range(tiles):
        outbox_ref[rows + TILE * i : rows + TILE * i + TILE, :] = current_t[:, TILE * i : TILE * i + TILE]


def factor_kernel(tiles, part_ref, packed_ref, initial_ref, outbox_ref, gram_ref):
    @pl.when(part_ref[0] == 0)
    def _():
        write_triangle(packed_ref, outbox_ref, tiles)

    @pl.when(part_ref[0] != 0)
    def _():
        write_basis(packed_ref, initial_ref, outbox_ref, gram_ref, tiles)


def closing_kernel(
    tiles, part_ref, outbox_ref, inbox_ref, unfold_ref, core_ref, basis_ref, triangle_ref, zero_ref, semaphores
):
    def close(triangle_box, basis_box):
        places = block_places(tiles)
        rows = basis_ref.shape[0]
        copies = [(basis_box.at[pl.ds(0, rows)], basis_ref)]
        for i in range(tiles):
            for j in range(tiles):
                at = places.get((i, j))
                source = zero_ref if at is None else triangle_box.at[pl.ds(TILE * at, TILE)]
                copies.append((source, triangle_ref.at[pl.ds(TILE * i, TILE), pl.ds(TILE * j, TILE)]))
        copies = [
            pltpu.make_async_copy(source, target, semaphores.at[n]) for n, (source, target) in enumerate(copies)
        ]
        for copy in copies:
            copy.start()
        current_t = jnp.concatenate(
            [basis_box[rows + TILE * i : rows + TILE * i + TILE, :] for i in range(tiles)], axis=1
        )
        core_flat = matmul(current_t, unfold_ref[...])
        cells = core_ref.shape[2]
        for slab in range(core_ref.shape[1]):
            core_ref[:, slab, :] = core_flat[:, slab * cells : slab * cells + cells]
        for copy in copies:
            copy.wait()

    zero_ref[...] = jnp.zeros_like(zero_ref)

    @pl.when(part_ref[0] == 0)
    def _():
        close(outbox_ref, inbox_ref)

    @pl.when(part_ref[0] != 0)
    def _():
        close(inbox_ref, outbox_ref)


VMEM_LIMIT = 32 * 2**20
WHOLE_VMEM = 63 * 2**20


def factors(packed, initial, part):
    rows, keep = initial.shape
    tiles = rows // TILE
    vmem = pl.BlockSpec(memory_space=pltpu.VMEM)
    return pl.pallas_call(
        functools.partial(factor_kernel, tiles),
        out_shape=jax.ShapeDtypeStruct((max(TILE * len(block_places(tiles)), rows + tiles * keep), TILE), jnp.float32),
        in_specs=[pl.BlockSpec(memory_space=pltpu.SMEM), vmem, vmem],
        out_specs=vmem,
        scratch_shapes=[pltpu.VMEM((rows, rows), jnp.float32)],
        compiler_params=pltpu.CompilerParams(vmem_limit_bytes=VMEM_LIMIT),
    )(part, packed, initial)


def finished(packed, initial, unfold, slab_count):
    rows, keep = initial.shape
    if lax.axis_size("col") % 2 == 0:
        part = jnp.full((1,), lax.axis_index("col") % 2, jnp.int32)
        outbox = factors(packed, initial, part)
        inbox = exchanged(outbox, "col", 1)
    else:
        part = jnp.zeros((1,), jnp.int32)
        outbox = factors(packed, initial, part)
        inbox = factors(packed, initial, part + 1)
    vmem = pl.BlockSpec(memory_space=pltpu.VMEM)
    return pl.pallas_call(
        functools.partial(closing_kernel, rows // TILE),
        out_shape=[
            jax.ShapeDtypeStruct((keep, slab_count, unfold.shape[1] // slab_count), jnp.float32),
            jax.ShapeDtypeStruct((rows, keep), jnp.float32),
            jax.ShapeDtypeStruct((rows, rows), jnp.float32),
        ],
        in_specs=[pl.BlockSpec(memory_space=pltpu.SMEM), vmem, vmem, vmem],
        out_specs=[vmem, pl.BlockSpec(memory_space=pl.ANY), pl.BlockSpec(memory_space=pl.ANY)],
        scratch_shapes=[
            pltpu.VMEM((TILE, TILE), jnp.float32),
            pltpu.SemaphoreType.DMA((1 + (rows // TILE) ** 2,)),
        ],
        compiler_params=pltpu.CompilerParams(vmem_limit_bytes=VMEM_LIMIT),
    )(part, outbox, inbox, unfold)


def blocks_kernel(tensor_ref, blocks_ref, read_ref, written_ref, read_done, write_done):
    chunks, rows, slab_count, _ = read_ref.shape
    count, columns = blocks_ref.shape[0], blocks_ref.shape[2]
    cells = columns // slab_count
    spans = [pl.ds(rows * n, rows) for n in range(chunks)]
    reads = [
        pltpu.make_async_copy(tensor_ref.at[span], read_ref.at[n], read_done.at[n]) for n, span in enumerate(spans)
    ]
    writes = [
        pltpu.make_async_copy(written_ref.at[n], blocks_ref.at[:, span, :], write_done.at[n])
        for n, span in enumerate(spans)
    ]
    for read in reads:
        read.start()
    for n in range(chunks):
        reads[n].wait()
        for part in range(count):
            for slab in range(slab_count):
                written_ref[n, part, :, slab * cells : slab * cells + cells] = read_ref[
                    n, :, slab, part * cells : part * cells + cells
                ]
        writes[n].start()
    for write in writes:
        write.wait()


def blocks_of(tensor, count):
    rows, slab_count, width = tensor.shape
    columns = slab_count * width // count
    chunk = SUB if rows % SUB == 0 else rows
    chunks = rows // chunk
    hbm = pl.BlockSpec(memory_space=pltpu.HBM)
    return pl.pallas_call(
        blocks_kernel,
        out_shape=jax.ShapeDtypeStruct((count, rows, columns), jnp.float32),
        in_specs=[hbm],
        out_specs=hbm,
        scratch_shapes=[
            pltpu.VMEM((chunks, chunk, slab_count, width), jnp.float32),
            pltpu.VMEM((chunks, count, chunk, columns), jnp.float32),
            pltpu.SemaphoreType.DMA((chunks,)),
            pltpu.SemaphoreType.DMA((chunks,)),
        ],
        compiler_params=pltpu.CompilerParams(vmem_limit_bytes=WHOLE_VMEM),
    )(tensor)


def gram_kernel(scale, half_ref, unfold_ref, packed_ref):
    tiles = unfold_ref.shape[0] // TILE
    row = lax.broadcasted_iota(jnp.int32, (TILE, TILE), 0)
    lane = lax.broadcasted_iota(jnp.int32, (TILE, TILE), 1)

    def make(offsets, doubles, base):
        wanted = set(offsets) | {(i, i) for pair in doubles for i in pair}
        blocks = {}
        for i in sorted({i for i, _ in wanted}):
            columns = sorted(j for first, j in wanted if first == i)
            left = unfold_ref[TILE * i : TILE * i + TILE, :]
            products = matmul_nt(left, unfold_ref[TILE * columns[0] : TILE * columns[-1] + TILE, :]) * scale
            for j in columns:
                start = TILE * (j - columns[0])
                blocks[i, j] = products[:, start : start + TILE]
        for pair, at in offsets.items():
            packed_ref[at - base : at - base + TILE, :] = blocks[pair]
        for (i, j), (at, line) in doubles.items():
            packed_ref[at - base : at - base + TILE, :] = jnp.where(lane >= row, blocks[i, i], blocks[j, j])
            diagonal = jnp.sum(jnp.where(lane == row, blocks[j, j], 0.0), axis=0, keepdims=True)
            packed_ref[line - base : line - base + 1, :] = diagonal

    for half, (offsets, doubles, base) in enumerate(packing(tiles)[0]):

        @pl.when(half_ref[0] == half)
        def _(offsets=offsets, doubles=doubles, base=base):
            lines = packed_ref.shape[0] - SPARE
            packed_ref[lines:, :] = jnp.zeros((SPARE, TILE), jnp.float32)
            make(offsets, doubles, base)


def gram_blocks(unfold, scale, half):
    rows, columns = unfold.shape
    _, length = packing(rows // TILE)
    vmem = pl.BlockSpec(memory_space=pltpu.VMEM)
    return pl.pallas_call(
        functools.partial(gram_kernel, scale),
        out_shape=jax.ShapeDtypeStruct((length, TILE), jnp.float32),
        in_specs=[pl.BlockSpec(memory_space=pltpu.SMEM), vmem],
        out_specs=vmem,
        compiler_params=pltpu.CompilerParams(vmem_limit_bytes=VMEM_LIMIT),
        cost_estimate=pl.CostEstimate(
            flops=2 * length * TILE * columns, bytes_accessed=4 * rows * columns, transcendentals=0
        ),
    )(jnp.full((1,), half, jnp.int32), unfold)


def local(tensor, initial):
    mode_size = lax.axis_size("mode")
    row_part, slab_count, width = tensor.shape
    row_count = row_part * mode_size
    column_total = slab_count * width * lax.axis_size("col")
    regrouped = lax.all_to_all(blocks_of(tensor, mode_size), "mode", split_axis=0, concat_axis=0, tiled=True)
    unfold = regrouped.reshape(row_count, slab_count * width // mode_size)
    scale = 1.0 / column_total
    if lax.axis_size("col") % 2:
        packed = summed(jnp.concatenate([gram_blocks(unfold, scale, half) for half in range(2)]))
    else:
        half = lax.axis_index("col") % 2
        other = gram_blocks(unfold, scale, 1 - half)
        packed = summed(gram_blocks(unfold, scale, half), other)
    return finished(packed, initial, unfold, slab_count)


def solution(mesh):
    return jax.shard_map(
        local,
        mesh=mesh,
        in_specs=(P("mode", "col", None), P()),
        out_specs=(P(None, "col", "mode"), P(), P()),
        check_vma=False,
    )
```

```python
import functools

import jax
import jax.numpy as jnp
from jax import lax
from jax.experimental import pallas as pl
from jax.experimental.pallas import tpu as pltpu
from jax.sharding import PartitionSpec as P

ITERS = 3
TILE = 128
SUB = 8
SPARE = 32
PANEL = 2

precise = lax.Precision.HIGHEST


def matmul(left, right):
    return jnp.dot(left, right, precision=precise, preferred_element_type=jnp.float32)


def matmul_tn(left, right):
    return lax.dot_general(
        left, right, (((0,), (0,)), ((), ())), precision=precise, preferred_element_type=jnp.float32
    )


def matmul_nt(left, right):
    return lax.dot_general(
        left, right, (((1,), (1,)), ((), ())), precision=precise, preferred_element_type=jnp.float32
    )


def exchanged(value, axis, distance):
    pairs = [(source, source ^ distance) for source in range(lax.axis_size(axis))]
    return lax.ppermute(value, axis, pairs)


def scattered_sum(value, axis, group):
    place = lax.axis_index(axis) % group
    rows = value.shape[0] // group
    total = lax.dynamic_slice_in_dim(value, place * rows, rows)
    parts = [
        exchanged(lax.dynamic_slice_in_dim(value, (place ^ distance) * rows, rows), axis, distance)
        for distance in reversed(range(1, group))
    ]
    for part in parts:
        total = total + part
    return total


def gathered(value, axis, group):
    place = lax.axis_index(axis) % group
    rows = value.shape[0]
    whole = jnp.zeros((group * rows,) + value.shape[1:], value.dtype)
    whole = lax.dynamic_update_slice_in_dim(whole, value, place * rows, 0)
    for distance in reversed(range(1, group)):
        part = exchanged(value, axis, distance)
        whole = lax.dynamic_update_slice_in_dim(whole, part, (place ^ distance) * rows, 0)
    return whole


def summed(share, other_share=None):
    mode_size, col_size = lax.axis_size("mode"), lax.axis_size("col")
    mode_group = min(4, mode_size)
    value = share if other_share is None else share + exchanged(other_share, "col", 1)
    value = scattered_sum(value, "mode", mode_group)
    distance = mode_group
    while distance < mode_size:
        value = value + exchanged(value, "mode", distance)
        distance *= 2
    distance = 1 if other_share is None else 2
    while distance < col_size:
        value = value + exchanged(value, "col", distance)
        distance *= 2
    value = gathered(value, "mode", mode_group)
    return value if other_share is None else gathered(value, "col", 2)


def row_of(tile, index):
    return jnp.broadcast_to(tile[index : index + 1, :], tile.shape)


def lane_of(tile, index):
    return jnp.take_along_axis(tile, jnp.full(tile.shape, index, jnp.int32), axis=1)


def factored(block, with_upper):
    side = block.shape[0]
    count = side // SUB
    width = PANEL * SUB
    row = lax.broadcasted_iota(jnp.int32, (SUB, side), 0)
    lane = lax.broadcasted_iota(jnp.int32, (SUB, side), 1)
    tiles = [block[SUB * t : SUB * t + SUB, :] for t in range(count)]
    scales = [None] * count
    members = range(PANEL)
    for first in range(0, count, PANEL):
        base = first * SUB
        inside = (lane >= base) & (lane < base + width)
        columns = [[lane_of(tiles[first + h], base + j) for h in members] for j in range(width)]
        near = range(first + PANEL, min(first + 2 * PANEL, count))
        far = range(first + 2 * PANEL, count)
        below = {t: [lane_of(tiles[t], base + j) for j in range(width)] for t in near}
        panel = [tiles[first + h] for h in members]
        if far:
            sent = jnp.concatenate([jnp.where(lane >= base + width + width, panel[h], 0.0) for h in members])
        kept, scale = list(panel), [None] * PANEL
        for pivot in range(0, width, 2):
            own, place = divmod(pivot, SUB)
            reached = range(own, PANEL)
            here, next_row = row == place, row == place + 1
            at, next_at = lane == base + pivot, lane == base + pivot + 1
            left, right = columns[pivot], columns[pivot + 1]
            a, b = row_of(left[own], place), row_of(right[own], place)
            c = row_of(right[own], place + 1)
            over_a = pl.reciprocal(a, approx=True)
            over_det = pl.reciprocal(a * c - b * b, approx=True)
            left = {h: left[h] for h in reached}
            right = {h: right[h] for h in reached}
            left[own] = jnp.where(here, -1.0, jnp.where(next_row, 0.0, left[own]))
            right[own] = jnp.where(here, 0.0, jnp.where(next_row, -1.0, right[own]))
            factor = {h: (c * left[h] - b * right[h]) * over_det for h in reached}
            next_factor = {h: (a * right[h] - b * left[h]) * over_det for h in reached}

            def reduced_by(value, top, bottom, h):
                return value - factor[h] * top - next_factor[h] * bottom

            for j in range(pivot + 2, width):
                top, bottom = row_of(columns[j][own], place), row_of(columns[j][own], place + 1)
                for h in reached:
                    value = jnp.where(here | next_row, 0.0, columns[j][h]) if h == own else columns[j][h]
                    columns[j][h] = reduced_by(value, top, bottom, h)
            top, bottom = row_of(panel[own], place), row_of(panel[own], place + 1)
            following = jnp.where(at, 0.0, bottom) - (b * over_a) * jnp.where(at, 1.0, top)
            kept[own] = jnp.where(here, panel[own], jnp.where(next_row, following, kept[own]))
            scale[own] = jnp.where(here, over_a, jnp.where(next_row, a * over_det, scale[own] if place else 0.0))
            top = jnp.where(at, 1.0, jnp.where(next_at, 0.0, top))
            bottom = jnp.where(at, 0.0, jnp.where(next_at, 1.0, bottom))
            for h in reached:
                cleared = at | next_at
                if h == own:
                    cleared = cleared | here | next_row
                panel[h] = reduced_by(jnp.where(cleared, 0.0, panel[h]), top, bottom, h)
        for h in reversed(members):
            for later in range(h + 1, PANEL):
                start = base + SUB * later
                panel[h] = jnp.where((lane >= start) & (lane < start + SUB), 0.0, panel[h])
                for m in range(SUB):
                    panel[h] = panel[h] - columns[SUB * later + m][h] * row_of(panel[later], m)
        for h in members:
            tiles[first + h] = kept[h]
            scales[first + h] = scale[h]
        if near:
            reduced = panel
            rows = [row_of(reduced[m // SUB], m % SUB) for m in range(width)]
            for t in near:
                even = jnp.where(inside, 0.0, tiles[t])
                odd = None
                for m in range(width):
                    term = below[t][m] * rows[m]
                    if m % 2:
                        odd = term if odd is None else odd + term
                    else:
                        even = even - term
                tiles[t] = even - odd
            if far:
                update = matmul_tn(sent, jnp.concatenate(reduced))
                for t in far:
                    tiles[t] = jnp.where(inside, 0.0, tiles[t]) - update[SUB * t : SUB * t + SUB]
    uppers, inverses = [], []
    for t in range(count):
        root = lax.rsqrt(scales[t]) * scales[t]
        scaled = tiles[t] * root
        diagonal = row + SUB * t
        uppers.append(jnp.where(lane >= diagonal, scaled, 0.0))
        inverses.append(jnp.where(lane < diagonal, scaled, jnp.where(lane == diagonal, root, 0.0)))
    return (jnp.concatenate(uppers) if with_upper else None), jnp.concatenate(inverses)


def block_places(tiles):
    return {
        pair: place for place, pair in enumerate((i, j) for i in range(tiles) for j in range(i, tiles))
    }


def packing(tiles):
    above = [(i, j) for i in range(tiles) for j in range(i + 1, tiles)]
    doubles = [(i, i + 1) for i in range(0, tiles, 2)]
    cut = len(doubles) // 2
    each = (len(above) + len(doubles)) // 2
    length = each * TILE + SPARE
    halves = []
    for half in range(2):
        base = half * length
        pairs = doubles[cut:] if half else doubles[:cut]
        blocks = above[each - cut :] if half else above[: each - cut]
        places = {pair: (base + TILE * n, base + each * TILE + n) for n, pair in enumerate(pairs)}
        offsets = {pair: base + TILE * (len(pairs) + n) for n, pair in enumerate(blocks)}
        halves.append((offsets, places, base))
    return halves, length


def unpacked(packed_ref, tiles):
    row = lax.broadcasted_iota(jnp.int32, (TILE, TILE), 0)
    lane = lax.broadcasted_iota(jnp.int32, (TILE, TILE), 1)
    blocks = {}
    for offsets, doubles, _ in packing(tiles)[0]:
        for pair, at in offsets.items():
            blocks[pair] = packed_ref[at : at + TILE, :]
        for (i, j), (at, line) in doubles.items():
            both = packed_ref[at : at + TILE, :]
            turned = both.T
            diagonal = jnp.broadcast_to(packed_ref[line : line + 1, :], (TILE, TILE))
            blocks[i, i] = jnp.where(lane >= row, both, turned)
            blocks[j, j] = jnp.where(lane < row, both, jnp.where(lane > row, turned, diagonal))
    return blocks


def write_triangle(packed_ref, outbox_ref, tiles):
    places = block_places(tiles)
    blocks = unpacked(packed_ref, tiles)
    for k in range(tiles):
        blocks[k, k], inverse = factored(blocks[k, k], True)
        for j in range(k + 1, tiles):
            blocks[k, j] = matmul(inverse, blocks[k, j])
        for j in range(k, tiles):
            at = places[k, j]
            outbox_ref[TILE * at : TILE * at + TILE, :] = blocks[k, j]
        for i in range(k + 1, tiles):
            for j in range(i, tiles):
                blocks[i, j] = blocks[i, j] - matmul_tn(blocks[k, i], blocks[k, j])


def write_basis(packed_ref, initial_ref, outbox_ref, gram_ref, tiles):
    for (i, j), block in unpacked(packed_ref, tiles).items():
        gram_ref[TILE * i : TILE * i + TILE, TILE * j : TILE * j + TILE] = block
        if i != j:
            gram_ref[TILE * j : TILE * j + TILE, TILE * i : TILE * i + TILE] = block.T
    product_t = matmul(initial_ref[...].T, gram_ref[...])
    for sweep in range(ITERS):
        inner = matmul_nt(product_t, product_t)
        if sweep < ITERS - 1:
            following = matmul(product_t, gram_ref[...])
        _, inverse = factored(inner, False)
        if sweep < ITERS - 1:
            product_t = matmul(inverse, following)
    current_t = matmul(inverse, product_t)
    rows = current_t.shape[1]
    outbox_ref[:rows, :] = current_t.T
    for i in range(tiles):
        outbox_ref[rows + TILE * i : rows + TILE * i + TILE, :] = current_t[:, TILE * i : TILE * i + TILE]


def factor_kernel(tiles, part_ref, packed_ref, initial_ref, outbox_ref, gram_ref):
    @pl.when(part_ref[0] == 0)
    def _():
        write_triangle(packed_ref, outbox_ref, tiles)

    @pl.when(part_ref[0] != 0)
    def _():
        write_basis(packed_ref, initial_ref, outbox_ref, gram_ref, tiles)


def closing_kernel(
    tiles, part_ref, outbox_ref, inbox_ref, unfold_ref, core_ref, basis_ref, triangle_ref, zero_ref, semaphores
):
    def close(triangle_box, basis_box):
        places = block_places(tiles)
        rows = basis_ref.shape[0]
        copies = [(basis_box.at[pl.ds(0, rows)], basis_ref)]
        for i in range(tiles):
            for j in range(tiles):
                at = places.get((i, j))
                source = zero_ref if at is None else triangle_box.at[pl.ds(TILE * at, TILE)]
                copies.append((source, triangle_ref.at[pl.ds(TILE * i, TILE), pl.ds(TILE * j, TILE)]))
        copies = [
            pltpu.make_async_copy(source, target, semaphores.at[n]) for n, (source, target) in enumerate(copies)
        ]
        for copy in copies:
            copy.start()
        current_t = jnp.concatenate(
            [basis_box[rows + TILE * i : rows + TILE * i + TILE, :] for i in range(tiles)], axis=1
        )
        core_flat = matmul(current_t, unfold_ref[...])
        cells = core_ref.shape[2]
        for slab in range(core_ref.shape[1]):
            core_ref[:, slab, :] = core_flat[:, slab * cells : slab * cells + cells]
        for copy in copies:
            copy.wait()

    zero_ref[...] = jnp.zeros_like(zero_ref)

    @pl.when(part_ref[0] == 0)
    def _():
        close(outbox_ref, inbox_ref)

    @pl.when(part_ref[0] != 0)
    def _():
        close(inbox_ref, outbox_ref)


VMEM_LIMIT = 32 * 2**20
WHOLE_VMEM = 63 * 2**20


def factors(packed, initial, part):
    rows, keep = initial.shape
    tiles = rows // TILE
    vmem = pl.BlockSpec(memory_space=pltpu.VMEM)
    return pl.pallas_call(
        functools.partial(factor_kernel, tiles),
        out_shape=jax.ShapeDtypeStruct((max(TILE * len(block_places(tiles)), rows + tiles * keep), TILE), jnp.float32),
        in_specs=[pl.BlockSpec(memory_space=pltpu.SMEM), vmem, vmem],
        out_specs=vmem,
        scratch_shapes=[pltpu.VMEM((rows, rows), jnp.float32)],
        compiler_params=pltpu.CompilerParams(vmem_limit_bytes=VMEM_LIMIT),
    )(part, packed, initial)


def finished(packed, initial, unfold, slab_count):
    rows, keep = initial.shape
    if lax.axis_size("col") % 2 == 0:
        part = jnp.full((1,), lax.axis_index("col") % 2, jnp.int32)
        outbox = factors(packed, initial, part)
        inbox = exchanged(outbox, "col", 1)
    else:
        part = jnp.zeros((1,), jnp.int32)
        outbox = factors(packed, initial, part)
        inbox = factors(packed, initial, part + 1)
    vmem = pl.BlockSpec(memory_space=pltpu.VMEM)
    return pl.pallas_call(
        functools.partial(closing_kernel, rows // TILE),
        out_shape=[
            jax.ShapeDtypeStruct((keep, slab_count, unfold.shape[1] // slab_count), jnp.float32),
            jax.ShapeDtypeStruct((rows, keep), jnp.float32),
            jax.ShapeDtypeStruct((rows, rows), jnp.float32),
        ],
        in_specs=[pl.BlockSpec(memory_space=pltpu.SMEM), vmem, vmem, vmem],
        out_specs=[vmem, pl.BlockSpec(memory_space=pl.ANY), pl.BlockSpec(memory_space=pl.ANY)],
        scratch_shapes=[
            pltpu.VMEM((TILE, TILE), jnp.float32),
            pltpu.SemaphoreType.DMA((1 + (rows // TILE) ** 2,)),
        ],
        compiler_params=pltpu.CompilerParams(vmem_limit_bytes=VMEM_LIMIT),
    )(part, outbox, inbox, unfold)


def blocks_kernel(tensor_ref, blocks_ref, read_ref, written_ref, read_done, write_done):
    chunks, rows, slab_count, _ = read_ref.shape
    count, columns = blocks_ref.shape[0], blocks_ref.shape[2]
    cells = columns // slab_count
    spans = [pl.ds(rows * n, rows) for n in range(chunks)]
    reads = [
        pltpu.make_async_copy(tensor_ref.at[span], read_ref.at[n], read_done.at[n]) for n, span in enumerate(spans)
    ]
    writes = [
        pltpu.make_async_copy(written_ref.at[n], blocks_ref.at[:, span, :], write_done.at[n])
        for n, span in enumerate(spans)
    ]
    for read in reads:
        read.start()
    for n in range(chunks):
        reads[n].wait()
        for part in range(count):
            for slab in range(slab_count):
                written_ref[n, part, :, slab * cells : slab * cells + cells] = read_ref[
                    n, :, slab, part * cells : part * cells + cells
                ]
        writes[n].start()
    for write in writes:
        write.wait()


def blocks_of(tensor, count):
    rows, slab_count, width = tensor.shape
    columns = slab_count * width // count
    chunk = SUB if rows % SUB == 0 else rows
    chunks = rows // chunk
    hbm = pl.BlockSpec(memory_space=pltpu.HBM)
    return pl.pallas_call(
        blocks_kernel,
        out_shape=jax.ShapeDtypeStruct((count, rows, columns), jnp.float32),
        in_specs=[hbm],
        out_specs=hbm,
        scratch_shapes=[
            pltpu.VMEM((chunks, chunk, slab_count, width), jnp.float32),
            pltpu.VMEM((chunks, count, chunk, columns), jnp.float32),
            pltpu.SemaphoreType.DMA((chunks,)),
            pltpu.SemaphoreType.DMA((chunks,)),
        ],
        compiler_params=pltpu.CompilerParams(vmem_limit_bytes=WHOLE_VMEM),
    )(tensor)


def gram_kernel(scale, half_ref, unfold_ref, packed_ref):
    tiles = unfold_ref.shape[0] // TILE
    row = lax.broadcasted_iota(jnp.int32, (TILE, TILE), 0)
    lane = lax.broadcasted_iota(jnp.int32, (TILE, TILE), 1)

    def make(offsets, doubles, base):
        wanted = set(offsets) | {(i, i) for pair in doubles for i in pair}
        blocks = {}
        for i in sorted({i for i, _ in wanted}):
            columns = sorted(j for first, j in wanted if first == i)
            left = unfold_ref[TILE * i : TILE * i + TILE, :]
            products = matmul_nt(left, unfold_ref[TILE * columns[0] : TILE * columns[-1] + TILE, :]) * scale
            for j in columns:
                start = TILE * (j - columns[0])
                blocks[i, j] = products[:, start : start + TILE]
        for pair, at in offsets.items():
            packed_ref[at - base : at - base + TILE, :] = blocks[pair]
        for (i, j), (at, line) in doubles.items():
            packed_ref[at - base : at - base + TILE, :] = jnp.where(lane >= row, blocks[i, i], blocks[j, j])
            diagonal = jnp.sum(jnp.where(lane == row, blocks[j, j], 0.0), axis=0, keepdims=True)
            packed_ref[line - base : line - base + 1, :] = diagonal

    for half, (offsets, doubles, base) in enumerate(packing(tiles)[0]):

        @pl.when(half_ref[0] == half)
        def _(offsets=offsets, doubles=doubles, base=base):
            lines = packed_ref.shape[0] - SPARE
            packed_ref[lines:, :] = jnp.zeros((SPARE, TILE), jnp.float32)
            make(offsets, doubles, base)


def gram_blocks(unfold, scale, half):
    rows, columns = unfold.shape
    _, length = packing(rows // TILE)
    vmem = pl.BlockSpec(memory_space=pltpu.VMEM)
    return pl.pallas_call(
        functools.partial(gram_kernel, scale),
        out_shape=jax.ShapeDtypeStruct((length, TILE), jnp.float32),
        in_specs=[pl.BlockSpec(memory_space=pltpu.SMEM), vmem],
        out_specs=vmem,
        compiler_params=pltpu.CompilerParams(vmem_limit_bytes=VMEM_LIMIT),
        cost_estimate=pl.CostEstimate(
            flops=2 * length * TILE * columns, bytes_accessed=4 * rows * columns, transcendentals=0
        ),
    )(jnp.full((1,), half, jnp.int32), unfold)


def local(tensor, initial):
    mode_size = lax.axis_size("mode")
    row_part, slab_count, width = tensor.shape
    row_count = row_part * mode_size
    column_total = slab_count * width * lax.axis_size("col")
    regrouped = lax.all_to_all(blocks_of(tensor, mode_size), "mode", split_axis=0, concat_axis=0, tiled=True)
    unfold = regrouped.reshape(row_count, slab_count * width // mode_size)
    scale = 1.0 / column_total
    if lax.axis_size("col") % 2:
        packed = summed(jnp.concatenate([gram_blocks(unfold, scale, half) for half in range(2)]))
    else:
        half = lax.axis_index("col") % 2
        other = gram_blocks(unfold, scale, 1 - half)
        packed = summed(gram_blocks(unfold, scale, half), other)
    return finished(packed, initial, unfold, slab_count)


def solution(mesh):
    return jax.shard_map(
        local,
        mesh=mesh,
        in_specs=(P("mode", "col", None), P()),
        out_specs=(P(None, "col", "mode"), P(), P()),
        check_vma=False,
    )
```
